512 devices in a mesh: noise: 16 (over x, z_lo), row: 32 (over z_hi, y, core).
Axes of the slice: x: 4, y: 4, z: 16 (z_hi: 4, z_lo: 4; z = z_hi * 4 + z_lo), core: 2. Of those that a mesh axis runs over, the one named last changes fastest.
Arguments:
- activations: bfloat16 [64, 2048, 768], P('noise', 'row'), may hold values from -6 to 6
- cond_scale: bfloat16 [64, 2048, 768], P('noise', 'row'), may hold values from 0.25 to 16
- cond_shift: bfloat16 [64, 2048, 768], P('noise', 'row'), may hold values from -4 to 4
- output_gate: bfloat16 [64, 2048, 768], P('noise', 'row'), may hold values from -8 to 8
- pair_repr: bfloat16 [2048, 2048, 128], P('row', 'noise'), may hold values from -6 to 6
- bias_weight: bfloat16 [128, 8], replicated, may hold values from -1.5 to 1.5
- query_weight: bfloat16 [768, 384], P('noise'), may hold values from -0.21875 to 0.21875
- query_bias: bfloat16 [384], replicated, may hold values from -4 to 4
- key_weight: bfloat16 [768, 384], P('noise'), may hold values from -0.21875 to 0.21875
- value_weight: bfloat16 [768, 384], P('noise'), may hold values from -0.21875 to 0.21875
- output_weight: bfloat16 [384, 768], P('noise'), may hold values from -0.3125 to 0.3125
- token_mask: int32 [64, 2048], P('noise', 'row'), may hold values from 0 to 1, as said below
Outputs:
- updated: bfloat16 [64, 2048, 768], P('noise', 'row')
The draws below stay inside these ranges and needn't reach their ends.
Inputs may be any that keep to these rules, and one draw needn't show every extreme that they name: `token_mask`: in each sample the tokens with mask 1 form a prefix of half of 2048 tokens or more, and some sample has all 2048 tokens.
All inputs are finite; a program needn't handle non-finite values.
Results may differ from the reference program's by a relative error of at most 0.012.
The reference program's roundings to bfloat16 on the way count: a program that leaves them out, or rounds other values in their place, can miss the bound.
Values may be sent and summed in bfloat16 or wider, within the bound.
A program may use at most 128 MiB of HBM per device.

```python
import math
import jax
import jax.numpy as jnp
from jax import lax

D = 768
HEADS = 8
HEAD_DIM = 48
PAIR_C = 128
ROW_TOKENS = 64
TOKENS = 2048
SAMPLES = 64


def draw_cond_scale(key, part):
    key = jax.random.fold_in(key, 11)
    key_scales = jax.random.fold_in(key, 0)
    scales = jnp.exp(jax.random.uniform(key_scales, (SAMPLES, TOKENS, D), jnp.float32, math.log(0.5), math.log(2.0)))
    return scales.astype(jnp.bfloat16)


def draw_token_mask(key, part):
    key = jax.random.fold_in(key, 23)
    key_lengths, key_full = jax.random.split(key)
    lengths = jax.random.randint(key_lengths, (SAMPLES,), TOKENS // 2, TOKENS + 1)
    full_sample = jax.random.randint(key_full, (), 0, SAMPLES)
    lengths = jnp.where(jnp.arange(SAMPLES) == full_sample, TOKENS, lengths)
    return (jnp.arange(TOKENS)[None, :] < lengths[:, None]).astype(jnp.int32)


def levels(key, extent, cuts, low, high):
    def one(dim, parts):
        draws = jax.random.uniform(jax.random.fold_in(jax.random.fold_in(key, 6), dim), (parts,), jnp.float32, low / len(cuts), high / len(cuts))
        return jnp.repeat(jnp.exp(draws), extent[dim] // parts).reshape((-1,) + (1,) * (len(extent) - dim - 1))

    factor_of = one(*cuts[0])
    for cut in cuts[1:]:
        factor_of = factor_of * one(*cut)
    return factor_of


def normal_values(own_key, shape, scale, most, shards=(), held_as=jnp.bfloat16):
    result = scale * jax.random.normal(own_key, shape, jnp.float32)
    if shards:
        result = result * levels(own_key, shape, shards, -0.22, 0.18)
    return jnp.clip(result, -most, most).astype(held_as)


def setup_inputs(seed: int = 0) -> dict:
    seeds = jax.random.split(jax.random.key(seed), 13)
    return {
        "activations": normal_values(seeds[0], (SAMPLES, TOKENS, D), 1.0, 6.0, ((0, 16), (1, 32))),
        "cond_scale": draw_cond_scale(jax.random.fold_in(seeds[12], 71), 0),
        "cond_shift": normal_values(seeds[2], (SAMPLES, TOKENS, D), 0.5, 4.0, ((0, 16), (1, 32))),
        "output_gate": normal_values(seeds[3], (SAMPLES, TOKENS, D), 1.5, 8.0, ((0, 16), (1, 32))),
        "pair_repr": normal_values(seeds[4], (TOKENS, TOKENS, PAIR_C), 1.0, 6.0, ((0, 32), (1, 16))),
        "bias_weight": normal_values(seeds[5], (PAIR_C, HEADS), 0.25, 1.5),
        "query_weight": normal_values(seeds[6], (D, HEADS * HEAD_DIM), D ** -0.5, 0.21875, ((0, 16),)),
        "query_bias": normal_values(seeds[7], (HEADS * HEAD_DIM,), 1.0, 4.0),
        "key_weight": normal_values(seeds[8], (D, HEADS * HEAD_DIM), D ** -0.5, 0.21875, ((0, 16),)),
        "value_weight": normal_values(seeds[9], (D, HEADS * HEAD_DIM), D ** -0.5, 0.21875, ((0, 16),)),
        "output_weight": normal_values(seeds[10], (HEADS * HEAD_DIM, D), (HEADS * HEAD_DIM) ** -0.5, 0.3125, ((0, 16),)),
        "token_mask": draw_token_mask(jax.random.fold_in(seeds[12], 71), 0),
    }


epsilon = 1e-05
masked_score = -1e+30

def layer_norm(tensor):
    average = lax.optimization_barrier(jnp.mean(tensor, axis=-1, keepdims=True))
    centred = tensor - average
    variance = lax.optimization_barrier(jnp.mean(centred * centred, axis=-1, keepdims=True))
    return centred * lax.rsqrt(variance + epsilon)

def reference(activations, cond_scale, cond_shift, output_gate, pair_repr, bias_weight, query_weight, query_bias, key_weight, value_weight, output_weight, token_mask):
    head_features = HEADS * HEAD_DIM
    normed = layer_norm(activations.astype(jnp.float32))
    shifted = (cond_scale.astype(jnp.float32) * normed + cond_shift.astype(jnp.float32)).astype(jnp.bfloat16)
    flat_rows = shifted.reshape(SAMPLES * TOKENS, D)
    queries = (jnp.dot(flat_rows, query_weight, preferred_element_type=jnp.float32) + query_bias.astype(jnp.float32)).astype(jnp.bfloat16)
    key_rows = jnp.dot(flat_rows, key_weight, preferred_element_type=jnp.float32).astype(jnp.bfloat16)
    value_rows = jnp.dot(flat_rows, value_weight, preferred_element_type=jnp.float32).astype(jnp.bfloat16)

    def bias_block(block_rows):
        return jnp.einsum('ijc,ch->hij', layer_norm(block_rows.astype(jnp.float32)), bias_weight.astype(jnp.float32), precision=lax.Precision.HIGHEST).astype(jnp.bfloat16)
    blocks = lax.map(bias_block, pair_repr.reshape(TOKENS // ROW_TOKENS, ROW_TOKENS, TOKENS, PAIR_C))
    pair_bias = blocks.transpose(1, 0, 2, 3).reshape(HEADS, TOKENS, TOKENS)
    score_factor = 1.0 / math.sqrt(HEAD_DIM)

    def one_sample(inputs):
        query_one, key_one, value_one, valid_one = inputs
        query_heads = query_one.reshape(TOKENS, HEADS, HEAD_DIM).astype(jnp.float32)
        key_heads = key_one.reshape(TOKENS, HEADS, HEAD_DIM).astype(jnp.float32)
        value_heads = value_one.reshape(TOKENS, HEADS, HEAD_DIM).astype(jnp.float32)
        scores = jnp.einsum('ihd,jhd->hij', query_heads, key_heads, precision=lax.Precision.HIGHEST) * score_factor + pair_bias.astype(jnp.float32)
        scores = jnp.where(valid_one[None, None, :] > 0, scores, masked_score)
        highest = lax.optimization_barrier(jnp.max(scores, axis=-1, keepdims=True))
        weights = jnp.exp(scores - highest)
        summed = lax.optimization_barrier(jnp.sum(weights, axis=-1, keepdims=True))
        rounded = lax.optimization_barrier(weights.astype(jnp.bfloat16))
        mixture = jnp.einsum('hij,jhd->hid', rounded.astype(jnp.float32), value_heads, precision=lax.Precision.HIGHEST) / summed
        return mixture.transpose(1, 0, 2).reshape(TOKENS, head_features).astype(jnp.bfloat16)
    attended = lax.map(one_sample, (queries.reshape(SAMPLES, TOKENS, head_features), key_rows.reshape(SAMPLES, TOKENS, head_features), value_rows.reshape(SAMPLES, TOKENS, head_features), token_mask))
    projected = jnp.dot(attended.reshape(SAMPLES * TOKENS, head_features), output_weight, preferred_element_type=jnp.float32).reshape(SAMPLES, TOKENS, D)
    return (activations.astype(jnp.float32) + jax.nn.sigmoid(output_gate.astype(jnp.float32)) * projected).astype(jnp.bfloat16)
```

```python
import functools
import math

import jax
import jax.numpy as jnp
from jax import lax
from jax.experimental import pallas as pl
from jax.experimental.pallas import tpu as pltpu
from jax.sharding import PartitionSpec as P

MESH = pl.DeviceIdType.MESH
f32 = jnp.float32
bf16 = jnp.bfloat16
epsilon = 1e-05
masked_score = -1e30
LOG2E = math.log2(math.e)

S = 4
T = 64
D = 768
F = 384
HW = 48
HALF = 192
WC = 640
KEYS = 2048
NT = (((1,), (1,)), ((), ()))


def iota(shape, dim):
    return lax.broadcasted_iota(jnp.int32, shape, dim)


def layer_norm(tensor):
    average = jnp.mean(tensor, axis=-1, keepdims=True)
    centred = tensor - average
    variance = jnp.mean(centred * centred, axis=-1, keepdims=True)
    return centred * lax.rsqrt(variance + epsilon)


def kernel(
    act_h, scale_h, shift_h, gate_h, pair_h, wb_ref, wq_ref, qb_ref, wk_ref, wv_ref, wo_ref, mask_ref,
    out_ref,
    act, scale, shift, gate, pair, local_sem,
    wg, wog, wop, qrow,
    sh, kvs, kvg, qs, qg,
    bt, btb, bc, bg, bf,
    mk, mks, mko, mg, mb,
    kaug, vaug, qaug,
    os_, og, xs, at,
    w_zl, w_x, wo_zl, wo_x, c_sem, b_zh, b_zl, b_x, m_zh, m_y, k_zh, q_zh, k_y, o_zh, a_c,
):
    noise, row = lax.axis_index("noise"), lax.axis_index("row")
    x, zl = noise // 4, lax.rem(noise, 4)
    zh, y, core = row // 8, lax.rem(row // 2, 4), lax.rem(row, 2)
    other = 1 - core

    def turn(v, d):
        return lax.rem(v + d + 4, 4)

    def dev(x=x, zl=zl, zh=zh, y=y, core=core):
        return (x * 4 + zl, zh * 8 + y * 2 + core)

    def remote(src, dst, sems, device):
        return pltpu.make_async_remote_copy(
            src_ref=src, dst_ref=dst, send_sem=sems[0], recv_sem=sems[1], device_id=device, device_id_type=MESH
        )

    def pair_of(sem, *index):
        return sem.at[(0, *index)], sem.at[(1, *index)]

    barrier = pltpu.get_barrier_semaphore()
    for d in (1, 2, 3):
        for where in (dev(zh=turn(zh, d)), dev(zl=turn(zl, d)), dev(x=turn(x, d)), dev(y=turn(y, d))):
            pl.semaphore_signal(barrier, inc=1, device_id=where, device_id_type=MESH)
    pl.semaphore_signal(barrier, inc=1, device_id=dev(core=other), device_id_type=MESH)

    loads = [
        pltpu.make_async_copy(source, target, local_sem.at[i])
        for i, (source, target) in enumerate(
            ((pair_h, pair), (act_h, act), (scale_h, scale), (shift_h, shift), (gate_h, gate))
        )
    ]
    for load in loads:
        load.start()

    def chosen(first):
        return ((iota((F, WC), 0) == iota((F, WC), 1) - first + HALF * core)
                & (iota((F, WC), 1) >= first) & (iota((F, WC), 1) < first + HALF)).astype(f32).astype(bf16)

    weights = (
        jnp.dot(wk_ref[...], chosen(0), preferred_element_type=f32)
        + jnp.dot(wv_ref[...], chosen(HALF), preferred_element_type=f32)
        + jnp.dot(wq_ref[...], chosen(2 * HALF), preferred_element_type=f32)
    )
    qrow[...] = jnp.dot(
        jnp.broadcast_to(qb_ref[...].astype(f32), (16, F)).astype(bf16), chosen(2 * HALF), preferred_element_type=f32
    )
    wg[noise] = weights.astype(bf16)
    wo = wo_ref[...].astype(f32)
    wog[noise] = jnp.concatenate([wo[:, :F], wo[:, F:]], axis=0).astype(bf16)
    lanes = (iota((T, 128), 1) == iota((T, 128), 0) + T * core).astype(f32).astype(bf16)
    mk[...] = jnp.zeros_like(mk)
    mk[0:S] = jnp.dot(mask_ref[...].astype(f32).astype(bf16), lanes, preferred_element_type=f32)
    mks[...] = mk[...].astype(bf16)

    pl.semaphore_wait(barrier, 13)

    w_zl_copies = [
        remote(wg.at[noise], wg.at[noise], pair_of(w_zl, d - 1), dev(zl=turn(zl, d))) for d in (1, 2, 3)
    ]
    for copy in w_zl_copies:
        copy.start()
    mask_core = remote(mks, mko, pair_of(c_sem, 0), dev(core=other))
    mask_core.start()

    wb = jnp.concatenate([wb_ref[...].astype(f32), jnp.zeros((128, 120), f32)], axis=1)
    wsum = jnp.sum(wb, axis=0, keepdims=True)
    wide = jnp.concatenate([wb, jnp.full((128, 128), 1.0 / 128, f32)], axis=1).astype(bf16)
    mean_at = jnp.where(iota((128, 128), 1) == 8, 1.0 / 128, 0.0).astype(bf16)
    loads[0].wait()

    def pair_rows(step, _):
        tile = pair[pl.ds(step * 8, 8)].reshape(1024, 128)
        both = jnp.dot(tile, wide, preferred_element_type=f32)
        mean = both[:, 128:]
        centred = tile.astype(f32) - mean
        square = (centred * centred).astype(bf16)
        table = both[:, :128] - mean * wsum + jnp.dot(square, mean_at, preferred_element_type=f32)
        for i in range(8):
            flipped = table[i * 128 : (i + 1) * 128].T
            bias = flipped[0:8] * lax.rsqrt(flipped[8:9] + epsilon)
            bt[:, pl.ds(step * 8 + i, 1), :] = bias.reshape(8, 1, 128)
        return 0

    lax.fori_loop(0, 8, pair_rows, 0)
    btb[...] = bt[...].astype(bf16).reshape(2, 4, T, 128)
    here = pl.ds(pl.multiple_of(core * T, T), T)
    bias_core = remote(btb.at[other], bc.at[:, here], pair_of(c_sem, 1), dev(core=other))
    bias_core.start()
    bc[:, here] = btb[core]

    for load in loads[1:4]:
        load.wait()

    def norm_rows(s, _):
        normed = layer_norm(act[s].astype(f32))
        sh[s, here] = (scale[s].astype(f32) * normed + shift[s].astype(f32)).astype(bf16)
        return 0

    lax.fori_loop(0, S, norm_rows, 0)
    shifted_core = remote(sh.at[:, here], sh.at[:, here], pair_of(c_sem, 2), dev(core=other))
    shifted_core.start()

    def weights_x(zl_from):
        block = x * 4 + zl_from
        copies = []
        for d in (1, 2, 3):
            copies.append(remote(wg.at[block], wg.at[block], pair_of(w_x, d - 1, zl_from), dev(x=turn(x, d))))
            copies[-1].start()
        return copies

    w_x_copies = weights_x(zl)
    for d in (1, 2, 3):
        source = turn(zl, -d)
        slot = wg.at[x * 4 + source]
        remote(slot, slot, pair_of(w_zl, d - 1), dev(zl=source)).wait_recv()
        w_x_copies += weights_x(source)

    there = pl.ds(pl.multiple_of(other * T, T), T)
    remote(btb.at[other], bc.at[:, there], pair_of(c_sem, 1), dev(core=other)).wait_recv()
    b_zh_copies = []
    for d in (1, 2, 3):
        to = turn(zh, d)
        b_zh_copies.append(remote(bc.at[to], bg.at[noise, zh], pair_of(b_zh, d - 1), dev(zh=to)))
        b_zh_copies[-1].start()
    bg[noise, zh] = bc[zh]
    mask_core.wait_recv()
    mg[y, zh] = mks[...] + mko[...]
    m_zh_copies = []
    for d in (1, 2, 3):
        m_zh_copies.append(remote(mg.at[y, zh], mg.at[y, zh], pair_of(m_zh, d - 1), dev(zh=turn(zh, d))))
        m_zh_copies[-1].start()
    wo_zl_copies = [
        remote(wog.at[noise], wog.at[noise], pair_of(wo_zl, d - 1), dev(zl=turn(zl, d))) for d in (1, 2, 3)
    ]
    for copy in wo_zl_copies:
        copy.start()

    def bias_x(zl_from):
        block = x * 4 + zl_from
        copies = []
        for d in (1, 2, 3):
            copies.append(remote(bg.at[block], bg.at[block], pair_of(b_x, d - 1, zl_from), dev(x=turn(x, d))))
            copies[-1].start()
        return copies

    for d in (1, 2, 3):
        source = turn(zh, -d)
        remote(bc.at[0], bg.at[noise, source], pair_of(b_zh, d - 1), dev(zh=source)).wait_recv()
    b_zl_copies = [
        remote(bg.at[noise], bg.at[noise], pair_of(b_zl, d - 1), dev(zl=turn(zl, d))) for d in (1, 2, 3)
    ]
    for copy in b_zl_copies:
        copy.start()
    b_x_copies = bias_x(zl)

    for d in (1, 2, 3):
        source = turn(zh, -d)
        slot = mg.at[y, source]
        remote(slot, slot, pair_of(m_zh, d - 1), dev(zh=source)).wait_recv()
    m_y_copies = []
    for d in (1, 2, 3):
        m_y_copies.append(remote(mg.at[y], mg.at[y], pair_of(m_y, d - 1), dev(y=turn(y, d))))
        m_y_copies[-1].start()

    remote(sh.at[:, there], sh.at[:, there], pair_of(c_sem, 2), dev(core=other)).wait_recv()
    for zl_from in range(4):
        for d in (1, 2, 3):
            slot = wg.at[turn(x, -d) * 4 + zl_from]
            remote(slot, slot, pair_of(w_x, d - 1, zl_from), dev(x=turn(x, -d))).wait_recv()

    def kv_copy(s, d):
        to = turn(zh, d)
        return remote(kvs.at[s, to], kvg.at[s, y, zh], pair_of(k_zh, s, d - 1), dev(zh=to))

    def q_copy(s, d):
        to = turn(zh, d)
        return remote(qs.at[s, to], qg.at[s, zh], pair_of(q_zh, s, d - 1), dev(zh=to))

    def project(s, _):
        rows = jnp.dot(sh[s], wg[...].reshape(D, WC), preferred_element_type=f32) + qrow[0:1]
        flipped = rows.T.astype(bf16)
        for h in range(4):
            kvs[s, h, 0:HW] = flipped[h * HW : (h + 1) * HW]
            kvs[s, h, HW : 2 * HW] = flipped[HALF + h * HW : HALF + (h + 1) * HW]
            qs[s, h] = flipped[2 * HALF + h * HW : 2 * HALF + (h + 1) * HW]
        for d in (1, 2, 3):
            kv_copy(s, d).start()
        for d in (1, 2, 3):
            q_copy(s, d).start()
        kvg[s, y, zh] = kvs[s, zh]
        qg[s, zh] = qs[s, zh]
        return 0

    lax.fori_loop(0, S, project, 0)

    def wo_x_send(zl_from):
        block = x * 4 + zl_from
        copies = []
        for d in (1, 2, 3):
            copies.append(remote(wog.at[block], wog.at[block], pair_of(wo_x, d - 1, zl_from), dev(x=turn(x, d))))
            copies[-1].start()
        return copies

    for d in (1, 2, 3):
        source = turn(zl, -d)
        slot = bg.at[x * 4 + source]
        remote(slot, slot, pair_of(b_zl, d - 1), dev(zl=source)).wait_recv()
        b_x_copies += bias_x(source)
    wo_x_copies = wo_x_send(zl)
    for d in (1, 2, 3):
        source = turn(zl, -d)
        slot = wog.at[x * 4 + source]
        remote(slot, slot, pair_of(wo_zl, d - 1), dev(zl=source)).wait_recv()
        wo_x_copies += wo_x_send(source)

    def ky_copy(s, d):
        return remote(kvg.at[s, y], kvg.at[s, y], pair_of(k_y, s, d - 1), dev(y=turn(y, d)))

    def forward(s):
        for d in (1, 2, 3):
            source = turn(zh, -d)
            remote(kvs.at[s, 0], kvg.at[s, y, source], pair_of(k_zh, s, d - 1), dev(zh=source)).wait_recv()
        for d in (1, 2, 3):
            ky_copy(s, d).start()

    forward(0)

    for d in (1, 2, 3):
        source = turn(y, -d)
        remote(mg.at[source], mg.at[source], pair_of(m_y, d - 1), dev(y=source)).wait_recv()
    for b in range(16):
        tokens = mg[b % 4, b // 4].astype(f32)
        for s in range(S):
            line = (tokens[s : s + 1] - 1.0) * (-masked_score)
            mb[s, :, b * 128 : (b + 1) * 128] = jnp.where(
                iota((16, 128), 0) == 0, jnp.broadcast_to(line, (16, 128)), 0.0
            ).astype(bf16)
    kaug[112:128] = jnp.zeros((16, KEYS), bf16)
    vaug[HW:128] = jnp.where(iota((80, KEYS), 0) == 0, 1.0, 0.0).astype(bf16)

    for zl_from in range(4):
        for d in (1, 2, 3):
            slot = bg.at[turn(x, -d) * 4 + zl_from]
            remote(slot, slot, pair_of(b_x, d - 1, zl_from), dev(x=turn(x, -d))).wait_recv()

    def widen(b, _):
        columns = pl.ds(pl.multiple_of(b * 128, 128), 128)
        bf[:, columns] = bg[b].reshape(512, 128).astype(f32) * LOG2E
        return 0

    lax.fori_loop(0, 16, widen, 0)

    def o_copy(s, d):
        to = turn(zh, d)
        return remote(os_.at[s, to], og.at[s, zh], pair_of(o_zh, s, d - 1), dev(zh=to))

    def attend(s):
        for d in (1, 2, 3):
            source = turn(zh, -d)
            remote(qs.at[s, 0], qg.at[s, source], pair_of(q_zh, s, d - 1), dev(zh=source)).wait_recv()
        for d in (1, 2, 3):
            source = turn(y, -d)
            slot = kvg.at[s, source]
            remote(slot, slot, pair_of(k_y, s, d - 1), dev(y=source)).wait_recv()
        for b in range(16):
            columns = slice(b * 128, (b + 1) * 128)
            block = kvg[s, b % 4, b // 4]
            kaug[0:HW, columns] = block[0:HW]
            kaug[HW : 2 * HW, columns] = block[0:HW]
            vaug[0:HW, columns] = block[HW : 2 * HW]
        kaug[96:112] = mb[s]
        for b in range(4):
            scaled = qg[s, b].astype(f32) * (LOG2E / math.sqrt(HW))
            high = scaled.astype(bf16).astype(f32)
            stacked = jnp.concatenate(
                [high, scaled - high, jnp.where(iota((32, 128), 0) == 0, 1.0, 0.0)], axis=0
            )
            qaug[b * 128 : (b + 1) * 128] = stacked.T.astype(bf16)

        def block_rows(r, _):
            rows = pl.ds(pl.multiple_of(r * 256, 256), 256)
            scores = jnp.dot(qaug[rows], kaug[...], preferred_element_type=f32) + bf[rows]
            highest = jnp.max(scores, axis=1, keepdims=True)
            probs = jnp.exp2(scores - highest).astype(bf16)
            mixed = lax.dot_general(probs, vaug[...], NT, preferred_element_type=f32).T
            attended = (mixed[0:HW] / mixed[HW : HW + 1]).astype(bf16)
            os_[s, 2 * r] = attended[:, 0:128]
            os_[s, 2 * r + 1] = attended[:, 128:256]
            return 0

        lax.fori_loop(0, 2, block_rows, 0)
        for d in (1, 2, 3):
            o_copy(s, d).start()
        og[s, zh] = os_[s, zh]

    def attention(s, _):
        forward(s + 1)
        attend(s)
        return 0

    lax.fori_loop(0, S - 1, attention, 0)
    attend(S - 1)

    for zl_from in range(4):
        for d in (1, 2, 3):
            slot = wog.at[turn(x, -d) * 4 + zl_from]
            remote(slot, slot, pair_of(wo_x, d - 1, zl_from), dev(x=turn(x, -d))).wait_recv()
    wop[...] = jnp.zeros_like(wop)
    for half in range(2):
        blocks = wog[8 * half : 8 * half + 8].astype(f32)
        for side in range(2):
            wop[half, 0:HALF, side * F : (side + 1) * F] = (
                blocks[:, side * 24 : (side + 1) * 24].reshape(HALF, F).astype(bf16)
            )

    def a_copy(s):
        return remote(xs.at[s], at.at[core, s], pair_of(a_c, s), dev(core=other))

    def collect(s, _):
        for d in (1, 2, 3):
            source = turn(zh, -d)
            remote(os_.at[s, 0], og.at[s, source], pair_of(o_zh, s, d - 1), dev(zh=source)).wait_recv()
        stacked = jnp.concatenate([og[s].astype(f32).reshape(HALF, 128), jnp.zeros((64, 128), f32)], axis=0)
        tokens = stacked.T.astype(bf16)
        first, second = tokens[0:T], tokens[T : 2 * T]
        xs[s] = jnp.where(core == 0, second.astype(f32), first.astype(f32)).astype(bf16)
        a_copy(s).start()
        at[core, s] = jnp.where(core == 0, first.astype(f32), second.astype(f32)).astype(bf16)
        return 0

    lax.fori_loop(0, S, collect, 0)
    loads[4].wait()

    def finish(s, _):
        slot = at.at[other, s]
        remote(xs.at[s], slot, pair_of(a_c, s), dev(core=other)).wait_recv()
        projected = jnp.dot(at[0, s], wop[0], preferred_element_type=f32) + jnp.dot(
            at[1, s], wop[1], preferred_element_type=f32
        )
        opened = jax.nn.sigmoid(gate[s].astype(f32))
        out_ref[s] = (act[s].astype(f32) + opened * projected).astype(bf16)
        return 0

    lax.fori_loop(0, S, finish, 0)

    mask_core.wait_send()
    bias_core.wait_send()
    shifted_core.wait_send()
    for copy in (
        w_zl_copies + w_x_copies + wo_zl_copies + wo_x_copies + b_zh_copies + b_zl_copies + b_x_copies
        + m_zh_copies + m_y_copies
    ):
        copy.wait_send()

    def drain(s, _):
        for d in (1, 2, 3):
            kv_copy(s, d).wait_send()
            q_copy(s, d).wait_send()
            ky_copy(s, d).wait_send()
            o_copy(s, d).wait_send()
        a_copy(s).wait_send()
        return 0

    lax.fori_loop(0, S, drain, 0)


def body(
    activations, cond_scale, cond_shift, output_gate, pair_repr, bias_weight, query_weight, query_bias, key_weight,
    value_weight, output_weight, token_mask,
):
    vmem = pl.BlockSpec(memory_space=pltpu.VMEM)
    any_ = pl.BlockSpec(memory_space=pl.ANY)
    dma = pltpu.SemaphoreType.DMA
    scratch = [
        *[pltpu.VMEM((S, T, D), bf16)] * 4,
        pltpu.VMEM((T, 128, 128), bf16),
        dma((5,)),
        pltpu.VMEM((16, HW, WC), bf16),
        pltpu.VMEM((16, HW, F), bf16),
        pltpu.VMEM((2, 256, D), bf16),
        pltpu.VMEM((16, WC), f32),
        pltpu.VMEM((S, 2 * T, D), bf16),
        pltpu.VMEM((S, 4, 2 * HW, 128), bf16),
        pltpu.VMEM((S, 4, 4, 2 * HW, 128), bf16),
        pltpu.VMEM((S, 4, HW, 128), bf16),
        pltpu.VMEM((S, 4, HW, 128), bf16),
        pltpu.VMEM((8, T, 128), f32),
        pltpu.VMEM((2, 4, T, 128), bf16),
        pltpu.VMEM((4, 2 * T, 128), bf16),
        pltpu.VMEM((16, 4, 128, 128), bf16),
        pltpu.VMEM((512, KEYS), f32),
        pltpu.VMEM((16, 128), f32),
        pltpu.VMEM((16, 128), bf16),
        pltpu.VMEM((16, 128), bf16),
        pltpu.VMEM((4, 4, 16, 128), bf16),
        pltpu.VMEM((S, 16, KEYS), bf16),
        pltpu.VMEM((128, KEYS), bf16),
        pltpu.VMEM((128, KEYS), bf16),
        pltpu.VMEM((512, 128), bf16),
        pltpu.VMEM((S, 4, HW, 128), bf16),
        pltpu.VMEM((S, 4, HW, 128), bf16),
        pltpu.VMEM((S, T, 256), bf16),
        pltpu.VMEM((2, S, T, 256), bf16),
        dma((2, 3)),
        dma((2, 3, 4)),
        dma((2, 3)),
        dma((2, 3, 4)),
        dma((2, 3)),
        dma((2, 3)),
        dma((2, 3)),
        dma((2, 3, 4)),
        dma((2, 3)),
        dma((2, 3)),
        dma((2, S, 3)),
        dma((2, S, 3)),
        dma((2, S, 3)),
        dma((2, S, 3)),
        dma((2, S)),
    ]
    return pl.pallas_call(
        kernel,
        out_shape=jax.ShapeDtypeStruct((S, T, D), bf16),
        in_specs=[any_] * 5 + [vmem] * 7,
        out_specs=vmem,
        scratch_shapes=scratch,
        compiler_params=pltpu.CompilerParams(
            collective_id=0, has_side_effects=True, vmem_limit_bytes=56 * 2**20
        ),
        cost_estimate=pl.CostEstimate(flops=2 * 10**9, bytes_accessed=5 * 10**6, transcendentals=4 * 10**6),
        name="pair_attention",
    )(
        activations, cond_scale, cond_shift, output_gate, pair_repr, bias_weight, query_weight,
        query_bias.reshape(1, F), key_weight, value_weight, output_weight, token_mask,
    )


def solution(mesh):
    return jax.shard_map(
        body,
        mesh=mesh,
        in_specs=(
            P("noise", "row", None),
            P("noise", "row", None),
            P("noise", "row", None),
            P("noise", "row", None),
            P("row", "noise", None),
            P(),
            P("noise", None),
            P(),
            P("noise", None),
            P("noise", None),
            P("noise", None),
            P("noise", "row"),
        ),
        out_specs=P("noise", "row", None),
        check_vma=False,
    )
```

```python
import functools
import math

import jax
import jax.numpy as jnp
from jax import lax
from jax.experimental import pallas as pl
from jax.experimental.pallas import tpu as pltpu
from jax.sharding import PartitionSpec as P

MESH = pl.DeviceIdType.MESH
f32 = jnp.float32
bf16 = jnp.bfloat16
epsilon = 1e-05
masked_score = -1e30
LOG2E = math.log2(math.e)

S = 4
T = 64
D = 768
F = 384
HW = 48
HALF = 192
WC = 640
KEYS = 2048
NT = (((1,), (1,)), ((), ()))


def iota(shape, dim):
    return lax.broadcasted_iota(jnp.int32, shape, dim)


def layer_norm(tensor):
    average = jnp.mean(tensor, axis=-1, keepdims=True)
    centred = tensor - average
    variance = jnp.mean(centred * centred, axis=-1, keepdims=True)
    return centred * lax.rsqrt(variance + epsilon)


def kernel(
    act_h, scale_h, shift_h, gate_h, pair_h, wb_ref, wq_ref, qb_ref, wk_ref, wv_ref, wo_ref, mask_ref,
    out_ref,
    act, scale, shift, gate, pair, local_sem,
    wg, wog, wop, qrow,
    sh, kvs, kvg, qs, qg,
    bt, btb, bc, bg, bf,
    mk, mks, mko, mg, mb,
    kaug, vaug, qaug,
    os_, og, xs, at,
    w_zl, w_x, wo_zl, wo_x, c_sem, b_zh, b_zl, b_x, m_zh, m_y, k_zh, q_zh, k_y, o_zh, a_c,
):
    noise, row = lax.axis_index("noise"), lax.axis_index("row")
    x, zl = noise // 4, lax.rem(noise, 4)
    zh, y, core = row // 8, lax.rem(row // 2, 4), lax.rem(row, 2)
    other = 1 - core

    def turn(v, d):
        return lax.rem(v + d + 4, 4)

    def dev(x=x, zl=zl, zh=zh, y=y, core=core):
        return (x * 4 + zl, zh * 8 + y * 2 + core)

    def remote(src, dst, sems, device):
        return pltpu.make_async_remote_copy(
            src_ref=src, dst_ref=dst, send_sem=sems[0], recv_sem=sems[1], device_id=device, device_id_type=MESH
        )

    def pair_of(sem, *index):
        return sem.at[(0, *index)], sem.at[(1, *index)]

    def hop(buffer, sems, way, origin):
        slot = buffer.at[x * 4 + origin]
        return remote(slot, slot, pair_of(sems, way, origin), dev(zl=turn(zl, 1 if way == 0 else -1)))

    def to_x(buffer, sems, origin, d):
        slot = buffer.at[x * 4 + origin]
        return remote(slot, slot, pair_of(sems, d - 1, origin), dev(x=turn(x, d)))

    def pass_on(buffer, z_sems, x_sems, origin, ways):
        for way in ways:

            @pl.when(zl < 3 if way == 0 else zl > 0)
            def _():
                hop(buffer, z_sems, way, origin).start()

        for d in (1, 2, 3):
            to_x(buffer, x_sems, origin, d).start()

    def line_step(buffer, z_sems, x_sems, k):
        @pl.when(zl >= k)
        def _():
            hop(buffer, z_sems, 0, zl - k).wait_recv()
            pass_on(buffer, z_sems, x_sems, zl - k, (0,))

        @pl.when(zl + k <= 3)
        def _():
            hop(buffer, z_sems, 1, zl + k).wait_recv()
            pass_on(buffer, z_sems, x_sems, zl + k, (1,))

    def line_drain(buffer, z_sems, x_sems):
        for origin in range(4):
            for d in (1, 2, 3):
                to_x(buffer, x_sems, origin, d).wait_send()

            @pl.when((zl < 3) & (zl >= origin))
            def _():
                hop(buffer, z_sems, 0, origin).wait_send()

            @pl.when((zl > 0) & (zl <= origin))
            def _():
                hop(buffer, z_sems, 1, origin).wait_send()

    barrier = pltpu.get_barrier_semaphore()
    for d in (1, 2, 3):
        for where in (dev(zh=turn(zh, d)), dev(zl=turn(zl, d)), dev(x=turn(x, d)), dev(y=turn(y, d))):
            pl.semaphore_signal(barrier, inc=1, device_id=where, device_id_type=MESH)
    pl.semaphore_signal(barrier, inc=1, device_id=dev(core=other), device_id_type=MESH)

    loads = [
        pltpu.make_async_copy(source, target, local_sem.at[i])
        for i, (source, target) in enumerate(
            ((pair_h, pair), (act_h, act), (scale_h, scale), (shift_h, shift), (gate_h, gate))
        )
    ]
    for load in loads:
        load.start()

    wb = jnp.concatenate([wb_ref[...].astype(f32), jnp.zeros((120, 128), f32)], axis=0).T
    wsum = jnp.sum(wb, axis=0, keepdims=True)
    wide = jnp.concatenate([wb, jnp.full((128, 128), 1.0 / 128, f32)], axis=1).astype(bf16)
    mean_at = jnp.where(iota((128, 128), 1) == 8, 1.0 / 128, 0.0).astype(bf16)
    loads[0].wait()

    def pair_rows(step, _):
        tile = pair[pl.ds(step * 8, 8)].reshape(1024, 128)
        both = jnp.dot(tile, wide, preferred_element_type=f32)
        mean = both[:, 128:]
        centred = tile.astype(f32) - mean
        square = (centred * centred).astype(bf16)
        table = both[:, :128] - mean * wsum + jnp.dot(square, mean_at, preferred_element_type=f32)
        for i in range(8):
            flipped = table[i * 128 : (i + 1) * 128].T
            bias = flipped[0:8] * lax.rsqrt(flipped[8:9] + epsilon)
            bt[:, pl.ds(step * 8 + i, 1), :] = bias.reshape(8, 1, 128)
        return 0

    lax.fori_loop(0, 8, pair_rows, 0)
    btb[...] = bt[...].astype(bf16).reshape(2, 4, T, 128)

    def chosen(first):
        return ((iota((F, WC), 0) == iota((F, WC), 1) - first + HALF * core)
                & (iota((F, WC), 1) >= first) & (iota((F, WC), 1) < first + HALF)).astype(f32).astype(bf16)

    weights = (
        jnp.dot(wk_ref[...], chosen(0), preferred_element_type=f32)
        + jnp.dot(wv_ref[...], chosen(HALF), preferred_element_type=f32)
        + jnp.dot(wq_ref[...], chosen(2 * HALF), preferred_element_type=f32)
    )
    qrow[...] = jnp.dot(
        jnp.broadcast_to(qb_ref[...].astype(f32).reshape(1, F), (16, F)).astype(bf16), chosen(2 * HALF), preferred_element_type=f32
    )
    wg[noise] = weights.astype(bf16)
    wo = wo_ref[...].astype(f32)
    wog[noise] = jnp.concatenate([wo[:, :F], wo[:, F:]], axis=0).astype(bf16)
    lanes = (iota((T, 128), 1) == iota((T, 128), 0) + T * core).astype(f32).astype(bf16)
    mk[...] = jnp.zeros_like(mk)
    mk[0:S] = jnp.dot(mask_ref[...].astype(f32).astype(bf16), lanes, preferred_element_type=f32)
    mks[...] = mk[...].astype(bf16)

    pl.semaphore_wait(barrier, 13)

    here = pl.ds(pl.multiple_of(core * T, T), T)
    bias_core = remote(btb.at[other], bc.at[:, here], pair_of(c_sem, 1), dev(core=other))
    bias_core.start()
    bc[:, here] = btb[core]
    pass_on(wg, w_zl, w_x, zl, (0, 1))
    mask_core = remote(mks, mko, pair_of(c_sem, 0), dev(core=other))
    mask_core.start()

    there = pl.ds(pl.multiple_of(other * T, T), T)
    remote(btb.at[other], bc.at[:, there], pair_of(c_sem, 1), dev(core=other)).wait_recv()
    b_zh_copies = []
    for d in (1, 2, 3):
        to = turn(zh, d)
        b_zh_copies.append(remote(bc.at[to], bg.at[noise, zh], pair_of(b_zh, d - 1), dev(zh=to)))
        b_zh_copies[-1].start()
    bg[noise, zh] = bc[zh]
    for load in loads[1:4]:
        load.wait()

    def norm_rows(s, _):
        normed = layer_norm(act[s].astype(f32))
        sh[s, here] = (scale[s].astype(f32) * normed + shift[s].astype(f32)).astype(bf16)
        return 0

    lax.fori_loop(0, S, norm_rows, 0)
    shifted_core = remote(sh.at[:, here], sh.at[:, here], pair_of(c_sem, 2), dev(core=other))
    shifted_core.start()

    for k in (1, 2, 3):
        line_step(wg, w_zl, w_x, k)

    mask_core.wait_recv()
    mg[y, zh] = mks[...] + mko[...]
    m_zh_copies = []
    for d in (1, 2, 3):
        m_zh_copies.append(remote(mg.at[y, zh], mg.at[y, zh], pair_of(m_zh, d - 1), dev(zh=turn(zh, d))))
        m_zh_copies[-1].start()

    remote(sh.at[:, there], sh.at[:, there], pair_of(c_sem, 2), dev(core=other)).wait_recv()
    for zl_from in range(4):
        for d in (1, 2, 3):
            slot = wg.at[turn(x, -d) * 4 + zl_from]
            remote(slot, slot, pair_of(w_x, d - 1, zl_from), dev(x=turn(x, -d))).wait_recv()

    def kv_copy(s, d):
        to = turn(zh, d)
        return remote(kvs.at[s, to], kvg.at[s, y, zh], pair_of(k_zh, s, d - 1), dev(zh=to))

    def q_copy(s, d):
        to = turn(zh, d)
        return remote(qs.at[s, to], qg.at[s, zh], pair_of(q_zh, s, d - 1), dev(zh=to))

    def ky_copy(s, d, e):
        slot = kvg.at[s, y, turn(zh, -e)]
        return remote(slot, slot, pair_of(k_y, s, d - 1, e), dev(y=turn(y, d)))

    def forward(s):
        for e in (1, 3, 2):
            source = turn(zh, -e)
            remote(kvs.at[s, 0], kvg.at[s, y, source], pair_of(k_zh, s, e - 1), dev(zh=source)).wait_recv()
            for d in (1, 2, 3):
                ky_copy(s, d, e).start()

    def project(s, _):
        rows = jnp.dot(sh[s], wg[...].reshape(D, WC), preferred_element_type=f32) + qrow[0:1]
        flipped = rows.T.astype(bf16)
        for h in range(4):
            kvs[s, h, 0:HW] = flipped[h * HW : (h + 1) * HW]
            kvs[s, h, HW : 2 * HW] = flipped[HALF + h * HW : HALF + (h + 1) * HW]
            qs[s, h] = flipped[2 * HALF + h * HW : 2 * HALF + (h + 1) * HW]
        kvg[s, y, zh] = kvs[s, zh]
        qg[s, zh] = qs[s, zh]
        return 0

    def exchange(s, _):
        for d in (1, 2, 3):
            kv_copy(s, d).start()
        for d in (1, 2, 3):
            q_copy(s, d).start()
        for d in (1, 2, 3):
            ky_copy(s, d, 0).start()
        return 0

    project(0, 0)
    exchange(0, 0)

    for d in (1, 2, 3):
        source = turn(zh, -d)
        remote(bc.at[0], bg.at[noise, source], pair_of(b_zh, d - 1), dev(zh=source)).wait_recv()
    pass_on(bg, b_zl, b_x, zl, (0, 1))
    lax.fori_loop(1, S, project, 0)
    line_step(bg, b_zl, b_x, 1)
    exchange(1, 0)
    for k in (2, 3):
        line_step(bg, b_zl, b_x, k)
    wo_zl_copies = [
        remote(wog.at[noise], wog.at[noise], pair_of(wo_zl, d - 1), dev(zl=turn(zl, d))) for d in (1, 2, 3)
    ]
    for copy in wo_zl_copies:
        copy.start()
    for d in (1, 2, 3):
        source = turn(zh, -d)
        slot = mg.at[y, source]
        remote(slot, slot, pair_of(m_zh, d - 1), dev(zh=source)).wait_recv()
    m_y_copies = []
    for d in (1, 2, 3):
        m_y_copies.append(remote(mg.at[y], mg.at[y], pair_of(m_y, d - 1), dev(y=turn(y, d))))
        m_y_copies[-1].start()


    def wo_x_send(zl_from):
        block = x * 4 + zl_from
        copies = []
        for d in (1, 2, 3):
            copies.append(remote(wog.at[block], wog.at[block], pair_of(wo_x, d - 1, zl_from), dev(x=turn(x, d))))
            copies[-1].start()
        return copies

    forward(0)
    exchange(2, 0)
    wo_x_copies = wo_x_send(zl)
    for d in (1, 2, 3):
        source = turn(zl, -d)
        slot = wog.at[x * 4 + source]
        remote(slot, slot, pair_of(wo_zl, d - 1), dev(zl=source)).wait_recv()
        wo_x_copies += wo_x_send(source)

    for d in (1, 2, 3):
        source = turn(y, -d)
        remote(mg.at[source], mg.at[source], pair_of(m_y, d - 1), dev(y=source)).wait_recv()
    for b in range(16):
        tokens = mg[b % 4, b // 4].astype(f32)
        for s in range(S):
            line = (tokens[s : s + 1] - 1.0) * (-masked_score)
            mb[s, :, b * 128 : (b + 1) * 128] = jnp.where(
                iota((16, 128), 0) == 0, jnp.broadcast_to(line, (16, 128)), 0.0
            ).astype(bf16)
    kaug[112:128] = jnp.zeros((16, KEYS), bf16)
    vaug[HW:128] = jnp.where(iota((80, KEYS), 0) == 0, 1.0, 0.0).astype(bf16)

    forward(1)
    exchange(3, 0)

    for zl_from in range(4):
        for d in (1, 2, 3):
            slot = bg.at[turn(x, -d) * 4 + zl_from]
            remote(slot, slot, pair_of(b_x, d - 1, zl_from), dev(x=turn(x, -d))).wait_recv()

    def widen(b, _):
        columns = pl.ds(pl.multiple_of(b * 128, 128), 128)
        bf[:, columns] = bg[b].reshape(512, 128).astype(f32) * LOG2E
        return 0

    lax.fori_loop(0, 16, widen, 0)

    def o_copy(s, d):
        to = turn(zh, d)
        return remote(os_.at[s, to], og.at[s, zh], pair_of(o_zh, s, d - 1), dev(zh=to))

    def attend(s):
        for d in (1, 2, 3):
            source = turn(zh, -d)
            remote(qs.at[s, 0], qg.at[s, source], pair_of(q_zh, s, d - 1), dev(zh=source)).wait_recv()
        for d in (1, 2, 3):
            source = turn(y, -d)
            for e in range(4):
                slot = kvg.at[s, source, turn(zh, -e)]
                remote(slot, slot, pair_of(k_y, s, d - 1, e), dev(y=source)).wait_recv()
        for b in range(16):
            columns = slice(b * 128, (b + 1) * 128)
            block = kvg[s, b % 4, b // 4]
            kaug[0:HW, columns] = block[0:HW]
            kaug[HW : 2 * HW, columns] = block[0:HW]
            vaug[0:HW, columns] = block[HW : 2 * HW]
        kaug[96:112] = mb[s]
        for b in range(4):
            scaled = qg[s, b].astype(f32) * (LOG2E / math.sqrt(HW))
            high = scaled.astype(bf16).astype(f32)
            stacked = jnp.concatenate(
                [high, scaled - high, jnp.where(iota((32, 128), 0) == 0, 1.0, 0.0)], axis=0
            )
            qaug[b * 128 : (b + 1) * 128] = stacked.T.astype(bf16)

        def block_rows(r, _):
            rows = pl.ds(pl.multiple_of(r * 256, 256), 256)
            scores = jnp.dot(qaug[rows], kaug[...], preferred_element_type=f32) + bf[rows]
            highest = jnp.max(scores, axis=1, keepdims=True)
            probs = jnp.exp2(scores - highest).astype(bf16)
            mixed = lax.dot_general(probs, vaug[...], NT, preferred_element_type=f32).T
            attended = (mixed[0:HW] / mixed[HW : HW + 1]).astype(bf16)
            os_[s, 2 * r] = attended[:, 0:128]
            os_[s, 2 * r + 1] = attended[:, 128:256]
            return 0

        lax.fori_loop(0, 2, block_rows, 0)
        for d in (1, 2, 3):
            o_copy(s, d).start()
        og[s, zh] = os_[s, zh]

    def attention(s, _):
        attend(s)

        @pl.when(s < 2)
        def _():
            forward(s + 2)

        return 0

    lax.fori_loop(0, S, attention, 0)

    for zl_from in range(4):
        for d in (1, 2, 3):
            slot = wog.at[turn(x, -d) * 4 + zl_from]
            remote(slot, slot, pair_of(wo_x, d - 1, zl_from), dev(x=turn(x, -d))).wait_recv()
    wop[...] = jnp.zeros_like(wop)
    for half in range(2):
        blocks = wog[8 * half : 8 * half + 8].astype(f32)
        for side in range(2):
            wop[half, 0:HALF, side * F : (side + 1) * F] = (
                blocks[:, side * 24 : (side + 1) * 24].reshape(HALF, F).astype(bf16)
            )

    def a_copy(s):
        return remote(xs.at[s], at.at[core, s], pair_of(a_c, s), dev(core=other))

    def collect(s, _):
        for d in (1, 2, 3):
            source = turn(zh, -d)
            remote(os_.at[s, 0], og.at[s, source], pair_of(o_zh, s, d - 1), dev(zh=source)).wait_recv()
        stacked = jnp.concatenate([og[s].astype(f32).reshape(HALF, 128), jnp.zeros((64, 128), f32)], axis=0)
        tokens = stacked.T.astype(bf16)
        first, second = tokens[0:T], tokens[T : 2 * T]
        xs[s] = jnp.where(core == 0, second.astype(f32), first.astype(f32)).astype(bf16)
        a_copy(s).start()
        at[core, s] = jnp.where(core == 0, first.astype(f32), second.astype(f32)).astype(bf16)
        return 0

    lax.fori_loop(0, S, collect, 0)
    loads[4].wait()

    def finish(s, _):
        slot = at.at[other, s]
        remote(xs.at[s], slot, pair_of(a_c, s), dev(core=other)).wait_recv()
        projected = jnp.dot(at[0, s], wop[0], preferred_element_type=f32) + jnp.dot(
            at[1, s], wop[1], preferred_element_type=f32
        )
        opened = jax.nn.sigmoid(gate[s].astype(f32))
        out_ref[s] = (act[s].astype(f32) + opened * projected).astype(bf16)
        return 0

    lax.fori_loop(0, S, finish, 0)

    mask_core.wait_send()
    bias_core.wait_send()
    shifted_core.wait_send()
    for copy in (wo_zl_copies + wo_x_copies + b_zh_copies + m_zh_copies + m_y_copies):
        copy.wait_send()

    line_drain(wg, w_zl, w_x)
    line_drain(bg, b_zl, b_x)

    def drain(s, _):
        for d in (1, 2, 3):
            kv_copy(s, d).wait_send()
            q_copy(s, d).wait_send()
            for e in range(4):
                ky_copy(s, d, e).wait_send()
            o_copy(s, d).wait_send()
        a_copy(s).wait_send()
        return 0

    lax.fori_loop(0, S, drain, 0)


def body(
    activations, cond_scale, cond_shift, output_gate, pair_repr, bias_weight, query_weight, query_bias, key_weight,
    value_weight, output_weight, token_mask,
):
    vmem = pl.BlockSpec(memory_space=pltpu.VMEM)
    any_ = pl.BlockSpec(memory_space=pl.ANY)
    dma = pltpu.SemaphoreType.DMA
    scratch = [
        *[pltpu.VMEM((S, T, D), bf16)] * 4,
        pltpu.VMEM((T, 128, 128), bf16),
        dma((5,)),
        pltpu.VMEM((16, HW, WC), bf16),
        pltpu.VMEM((16, HW, F), bf16),
        pltpu.VMEM((2, 256, D), bf16),
        pltpu.VMEM((16, WC), f32),
        pltpu.VMEM((S, 2 * T, D), bf16),
        pltpu.VMEM((S, 4, 2 * HW, 128), bf16),
        pltpu.VMEM((S, 4, 4, 2 * HW, 128), bf16),
        pltpu.VMEM((S, 4, HW, 128), bf16),
        pltpu.VMEM((S, 4, HW, 128), bf16),
        pltpu.VMEM((8, T, 128), f32),
        pltpu.VMEM((2, 4, T, 128), bf16),
        pltpu.VMEM((4, 2 * T, 128), bf16),
        pltpu.VMEM((16, 4, 128, 128), bf16),
        pltpu.VMEM((512, KEYS), f32),
        pltpu.VMEM((16, 128), f32),
        pltpu.VMEM((16, 128), bf16),
        pltpu.VMEM((16, 128), bf16),
        pltpu.VMEM((4, 4, 16, 128), bf16),
        pltpu.VMEM((S, 16, KEYS), bf16),
        pltpu.VMEM((128, KEYS), bf16),
        pltpu.VMEM((128, KEYS), bf16),
        pltpu.VMEM((512, 128), bf16),
        pltpu.VMEM((S, 4, HW, 128), bf16),
        pltpu.VMEM((S, 4, HW, 128), bf16),
        pltpu.VMEM((S, T, 256), bf16),
        pltpu.VMEM((2, S, T, 256), bf16),
        dma((2, 2, 4)),
        dma((2, 3, 4)),
        dma((2, 3)),
        dma((2, 3, 4)),
        dma((2, 3)),
        dma((2, 3)),
        dma((2, 2, 4)),
        dma((2, 3, 4)),
        dma((2, 3)),
        dma((2, 3)),
        dma((2, S, 3)),
        dma((2, S, 3)),
        dma((2, S, 3, 4)),
        dma((2, S, 3)),
        dma((2, S)),
    ]
    return pl.pallas_call(
        kernel,
        out_shape=jax.ShapeDtypeStruct((S, T, D), bf16),
        in_specs=[any_] * 5 + [vmem] * 7,
        out_specs=vmem,
        scratch_shapes=scratch,
        compiler_params=pltpu.CompilerParams(
            collective_id=0, has_side_effects=True, vmem_limit_bytes=56 * 2**20
        ),
        cost_estimate=pl.CostEstimate(flops=2 * 10**9, bytes_accessed=5 * 10**6, transcendentals=4 * 10**6),
        name="pair_attention",
    )(
        activations, cond_scale, cond_shift, output_gate, pair_repr, bias_weight.T, query_weight,
        query_bias, key_weight, value_weight, output_weight, token_mask,
    )


def solution(mesh):
    return jax.shard_map(
        body,
        mesh=mesh,
        in_specs=(
            P("noise", "row", None),
            P("noise", "row", None),
            P("noise", "row", None),
            P("noise", "row", None),
            P("row", "noise", None),
            P(),
            P("noise", None),
            P(),
            P("noise", None),
            P("noise", None),
            P("noise", None),
            P("noise", "row"),
        ),
        out_specs=P("noise", "row", None),
        check_vma=False,
    )
```

```python
import functools
import math

import jax
import jax.numpy as jnp
from jax import lax
from jax.experimental import pallas as pl
from jax.experimental.pallas import tpu as pltpu
from jax.sharding import PartitionSpec as P

MESH = pl.DeviceIdType.MESH
f32 = jnp.float32
bf16 = jnp.bfloat16
epsilon = 1e-05
masked_score = -1e30
LOG2E = math.log2(math.e)

S = 4
T = 64
D = 768
F = 384
HW = 48
HALF = 192
WC = 640
KEYS = 2048
NT = (((1,), (1,)), ((), ()))


def iota(shape, dim):
    return lax.broadcasted_iota(jnp.int32, shape, dim)


def layer_norm(tensor):
    average = jnp.mean(tensor, axis=-1, keepdims=True)
    centred = tensor - average
    variance = jnp.mean(centred * centred, axis=-1, keepdims=True)
    return centred * lax.rsqrt(variance + epsilon)


def kernel(
    act_h, scale_h, shift_h, gate_h, pair_h, wb_h, wq_h, qb_ref, wk_h, wv_h, wo_h, mask_h,
    out_h,
    act, scale, shift, gate, pair, wb_ref, wq_ref, wk_ref, wv_ref, wo_ref, mask_ref, out, local_sem, out_sem,
    wg, wog, wop, qrow,
    sh, kvs, kvg, qs, qg,
    bt, btb, bc, bg, bf,
    mk, mks, mko, mg, mb,
    kaug, vaug, qaug,
    os_, og, xs, at,
    w_zl, w_x, wo_zl, wo_x, c_sem, b_zh, b_zl, b_x, m_zh, m_y, k_zh, q_zh, k_y, o_zh, a_c,
):
    noise, row = lax.axis_index("noise"), lax.axis_index("row")
    x, zl = noise // 4, lax.rem(noise, 4)
    zh, y, core = row // 8, lax.rem(row // 2, 4), lax.rem(row, 2)
    other = 1 - core

    def turn(v, d):
        return lax.rem(v + d + 4, 4)

    def dev(x=x, zl=zl, zh=zh, y=y, core=core):
        return (x * 4 + zl, zh * 8 + y * 2 + core)

    def remote(src, dst, sems, device):
        return pltpu.make_async_remote_copy(
            src_ref=src, dst_ref=dst, send_sem=sems[0], recv_sem=sems[1], device_id=device, device_id_type=MESH
        )

    def pair_of(sem, *index):
        return sem.at[(0, *index)], sem.at[(1, *index)]

    def hop(buffer, sems, way, origin):
        slot = buffer.at[x * 4 + origin]
        return remote(slot, slot, pair_of(sems, way, origin), dev(zl=turn(zl, 1 if way == 0 else -1)))

    def to_x(buffer, sems, origin, d):
        slot = buffer.at[x * 4 + origin]
        return remote(slot, slot, pair_of(sems, d - 1, origin), dev(x=turn(x, d)))

    def pass_on(buffer, z_sems, x_sems, origin, ways):
        for way in ways:

            @pl.when(zl < 3 if way == 0 else zl > 0)
            def _():
                hop(buffer, z_sems, way, origin).start()

        for d in (1, 2, 3):
            to_x(buffer, x_sems, origin, d).start()

    def line_step(buffer, z_sems, x_sems, k):
        @pl.when(zl >= k)
        def _():
            hop(buffer, z_sems, 0, zl - k).wait_recv()
            pass_on(buffer, z_sems, x_sems, zl - k, (0,))

        @pl.when(zl + k <= 3)
        def _():
            hop(buffer, z_sems, 1, zl + k).wait_recv()
            pass_on(buffer, z_sems, x_sems, zl + k, (1,))

    def line_drain(buffer, z_sems, x_sems):
        for origin in range(4):
            for d in (1, 2, 3):
                to_x(buffer, x_sems, origin, d).wait_send()

            @pl.when((zl < 3) & (zl >= origin))
            def _():
                hop(buffer, z_sems, 0, origin).wait_send()

            @pl.when((zl > 0) & (zl <= origin))
            def _():
                hop(buffer, z_sems, 1, origin).wait_send()

    barrier = pltpu.get_barrier_semaphore()
    for d in (1, 2, 3):
        for where in (dev(zh=turn(zh, d)), dev(zl=turn(zl, d)), dev(x=turn(x, d)), dev(y=turn(y, d))):
            pl.semaphore_signal(barrier, inc=1, device_id=where, device_id_type=MESH)
    pl.semaphore_signal(barrier, inc=1, device_id=dev(core=other), device_id_type=MESH)

    loads = [
        pltpu.make_async_copy(source, target, local_sem.at[i])
        for i, (source, target) in enumerate(
            (
                (pair_h, pair), (wb_h, wb_ref), (wq_h, wq_ref), (wk_h, wk_ref), (wv_h, wv_ref), (wo_h, wo_ref),
                (mask_h, mask_ref), (act_h, act), (scale_h, scale), (shift_h, shift), (gate_h, gate),
            )
        )
    ]
    for load in loads:
        load.start()

    for load in loads[2:7]:
        load.wait()

    def chosen(first):
        return ((iota((F, WC), 0) == iota((F, WC), 1) - first + HALF * core)
                & (iota((F, WC), 1) >= first) & (iota((F, WC), 1) < first + HALF)).astype(f32).astype(bf16)

    weights = (
        jnp.dot(wk_ref[...], chosen(0), preferred_element_type=f32)
        + jnp.dot(wv_ref[...], chosen(HALF), preferred_element_type=f32)
        + jnp.dot(wq_ref[...], chosen(2 * HALF), preferred_element_type=f32)
    )
    qrow[...] = jnp.dot(
        jnp.broadcast_to(qb_ref[...].astype(f32).reshape(1, F), (16, F)).astype(bf16), chosen(2 * HALF), preferred_element_type=f32
    )
    wg[noise] = weights.astype(bf16)
    wo = wo_ref[...].astype(f32)
    wog[noise] = jnp.concatenate([wo[:, :F], wo[:, F:]], axis=0).astype(bf16)
    lanes = (iota((T, 128), 1) == iota((T, 128), 0) + T * core).astype(f32).astype(bf16)
    mk[...] = jnp.zeros_like(mk)
    mk[0:S] = jnp.dot(mask_ref[...].astype(f32).astype(bf16), lanes, preferred_element_type=f32)
    mks[...] = mk[...].astype(bf16)

    loads[1].wait()
    wb = jnp.concatenate([wb_ref[...].astype(f32), jnp.zeros((120, 128), f32)], axis=0).T
    wsum = jnp.sum(wb, axis=0, keepdims=True)
    wide = jnp.concatenate([wb, jnp.full((128, 128), 1.0 / 128, f32)], axis=1).astype(bf16)
    mean_at = jnp.where(iota((128, 128), 1) == 8, 1.0 / 128, 0.0).astype(bf16)
    loads[0].wait()

    def pair_rows(step, _):
        tile = pair[pl.ds(step * 8, 8)].reshape(1024, 128)
        both = jnp.dot(tile, wide, preferred_element_type=f32)
        mean = both[:, 128:]
        centred = tile.astype(f32) - mean
        square = (centred * centred).astype(bf16)
        table = both[:, :128] - mean * wsum + jnp.dot(square, mean_at, preferred_element_type=f32)
        for i in range(8):
            flipped = table[i * 128 : (i + 1) * 128].T
            bias = flipped[0:8] * lax.rsqrt(flipped[8:9] + epsilon)
            bt[:, pl.ds(step * 8 + i, 1), :] = bias.reshape(8, 1, 128)
        return 0

    lax.fori_loop(0, 4, pair_rows, 0)

    pl.semaphore_wait(barrier, 13)

    pass_on(wg, w_zl, w_x, zl, (0, 1))
    mask_core = remote(mks, mko, pair_of(c_sem, 0), dev(core=other))
    mask_core.start()

    lax.fori_loop(4, 6, pair_rows, 0)
    line_step(wg, w_zl, w_x, 1)
    lax.fori_loop(6, 8, pair_rows, 0)
    btb[...] = bt[...].astype(bf16).reshape(2, 4, T, 128)
    here = pl.ds(pl.multiple_of(core * T, T), T)
    bias_core = remote(btb.at[other], bc.at[:, here], pair_of(c_sem, 1), dev(core=other))
    bias_core.start()
    bc[:, here] = btb[core]
    line_step(wg, w_zl, w_x, 2)

    there = pl.ds(pl.multiple_of(other * T, T), T)
    remote(btb.at[other], bc.at[:, there], pair_of(c_sem, 1), dev(core=other)).wait_recv()
    b_zh_copies = []
    for d in (1, 2, 3):
        to = turn(zh, d)
        b_zh_copies.append(remote(bc.at[to], bg.at[noise, zh], pair_of(b_zh, d - 1), dev(zh=to)))
        b_zh_copies[-1].start()
    bg[noise, zh] = bc[zh]
    line_step(wg, w_zl, w_x, 3)
    for load in loads[7:10]:
        load.wait()

    def norm_rows(s, _):
        normed = layer_norm(act[s].astype(f32))
        sh[s, here] = (scale[s].astype(f32) * normed + shift[s].astype(f32)).astype(bf16)
        return 0

    lax.fori_loop(0, S, norm_rows, 0)
    shifted_core = remote(sh.at[:, here], sh.at[:, here], pair_of(c_sem, 2), dev(core=other))
    shifted_core.start()

    mask_core.wait_recv()
    mg[y, zh] = mks[...] + mko[...]
    m_zh_copies = []
    for d in (1, 2, 3):
        m_zh_copies.append(remote(mg.at[y, zh], mg.at[y, zh], pair_of(m_zh, d - 1), dev(zh=turn(zh, d))))
        m_zh_copies[-1].start()

    remote(sh.at[:, there], sh.at[:, there], pair_of(c_sem, 2), dev(core=other)).wait_recv()
    for zl_from in range(4):
        for d in (1, 2, 3):
            slot = wg.at[turn(x, -d) * 4 + zl_from]
            remote(slot, slot, pair_of(w_x, d - 1, zl_from), dev(x=turn(x, -d))).wait_recv()

    def kv_copy(s, d):
        to = turn(zh, d)
        return remote(kvs.at[s, to], kvg.at[s, y, zh], pair_of(k_zh, s, d - 1), dev(zh=to))

    def q_copy(s, d):
        to = turn(zh, d)
        return remote(qs.at[s, to], qg.at[s, zh], pair_of(q_zh, s, d - 1), dev(zh=to))

    def ky_copy(s, d, e):
        slot = kvg.at[s, y, turn(zh, -e)]
        return remote(slot, slot, pair_of(k_y, s, d - 1, e), dev(y=turn(y, d)))

    def forward(s):
        for e in (1, 3, 2):
            source = turn(zh, -e)
            remote(kvs.at[s, 0], kvg.at[s, y, source], pair_of(k_zh, s, e - 1), dev(zh=source)).wait_recv()
            for d in (1, 2, 3):
                ky_copy(s, d, e).start()

    def project(s, _):
        rows = jnp.dot(sh[s], wg[...].reshape(D, WC), preferred_element_type=f32) + qrow[0:1]
        flipped = rows.T.astype(bf16)
        for h in range(4):
            kvs[s, h, 0:HW] = flipped[h * HW : (h + 1) * HW]
            kvs[s, h, HW : 2 * HW] = flipped[HALF + h * HW : HALF + (h + 1) * HW]
            qs[s, h] = flipped[2 * HALF + h * HW : 2 * HALF + (h + 1) * HW]
        kvg[s, y, zh] = kvs[s, zh]
        qg[s, zh] = qs[s, zh]
        return 0

    def exchange(s, _):
        for d in (1, 2, 3):
            kv_copy(s, d).start()
        for d in (1, 2, 3):
            q_copy(s, d).start()
        for d in (1, 2, 3):
            ky_copy(s, d, 0).start()
        return 0

    project(0, 0)
    exchange(0, 0)

    for d in (1, 2, 3):
        source = turn(zh, -d)
        remote(bc.at[0], bg.at[noise, source], pair_of(b_zh, d - 1), dev(zh=source)).wait_recv()
    pass_on(bg, b_zl, b_x, zl, (0, 1))
    lax.fori_loop(1, S, project, 0)
    line_step(bg, b_zl, b_x, 1)
    exchange(1, 0)
    for k in (2, 3):
        line_step(bg, b_zl, b_x, k)
    wo_zl_copies = [
        remote(wog.at[noise], wog.at[noise], pair_of(wo_zl, d - 1), dev(zl=turn(zl, d))) for d in (1, 2, 3)
    ]
    for copy in wo_zl_copies:
        copy.start()
    for d in (1, 2, 3):
        source = turn(zh, -d)
        slot = mg.at[y, source]
        remote(slot, slot, pair_of(m_zh, d - 1), dev(zh=source)).wait_recv()
    m_y_copies = []
    for d in (1, 2, 3):
        m_y_copies.append(remote(mg.at[y], mg.at[y], pair_of(m_y, d - 1), dev(y=turn(y, d))))
        m_y_copies[-1].start()


    def wo_x_send(zl_from):
        block = x * 4 + zl_from
        copies = []
        for d in (1, 2, 3):
            copies.append(remote(wog.at[block], wog.at[block], pair_of(wo_x, d - 1, zl_from), dev(x=turn(x, d))))
            copies[-1].start()
        return copies

    forward(0)
    exchange(2, 0)
    wo_x_copies = wo_x_send(zl)
    for d in (1, 2, 3):
        source = turn(zl, -d)
        slot = wog.at[x * 4 + source]
        remote(slot, slot, pair_of(wo_zl, d - 1), dev(zl=source)).wait_recv()
        wo_x_copies += wo_x_send(source)

    for d in (1, 2, 3):
        source = turn(y, -d)
        remote(mg.at[source], mg.at[source], pair_of(m_y, d - 1), dev(y=source)).wait_recv()
    for b in range(16):
        tokens = mg[b % 4, b // 4].astype(f32)
        for s in range(S):
            line = (tokens[s : s + 1] - 1.0) * (-masked_score)
            mb[s, :, b * 128 : (b + 1) * 128] = jnp.where(
                iota((16, 128), 0) == 0, jnp.broadcast_to(line, (16, 128)), 0.0
            ).astype(bf16)
    kaug[112:128] = jnp.zeros((16, KEYS), bf16)
    vaug[HW:128] = jnp.where(iota((80, KEYS), 0) == 0, 1.0, 0.0).astype(bf16)

    forward(1)
    exchange(3, 0)

    for zl_from in range(4):
        for d in (1, 2, 3):
            slot = bg.at[turn(x, -d) * 4 + zl_from]
            remote(slot, slot, pair_of(b_x, d - 1, zl_from), dev(x=turn(x, -d))).wait_recv()

    def widen(b, _):
        columns = pl.ds(pl.multiple_of(b * 128, 128), 128)
        bf[:, columns] = bg[b].reshape(512, 128).astype(f32) * LOG2E
        return 0

    lax.fori_loop(0, 16, widen, 0)

    def o_copy(s, d):
        to = turn(zh, d)
        return remote(os_.at[s, to], og.at[s, zh], pair_of(o_zh, s, d - 1), dev(zh=to))

    def attend(s):
        for d in (1, 2, 3):
            source = turn(zh, -d)
            remote(qs.at[s, 0], qg.at[s, source], pair_of(q_zh, s, d - 1), dev(zh=source)).wait_recv()
        for d in (1, 2, 3):
            source = turn(y, -d)
            for e in range(4):
                slot = kvg.at[s, source, turn(zh, -e)]
                remote(slot, slot, pair_of(k_y, s, d - 1, e), dev(y=source)).wait_recv()
        for b in range(16):
            columns = slice(b * 128, (b + 1) * 128)
            block = kvg[s, b % 4, b // 4]
            kaug[0:HW, columns] = block[0:HW]
            kaug[HW : 2 * HW, columns] = block[0:HW]
            vaug[0:HW, columns] = block[HW : 2 * HW]
        kaug[96:112] = mb[s]
        for b in range(4):
            scaled = qg[s, b].astype(f32) * (LOG2E / math.sqrt(HW))
            high = scaled.astype(bf16).astype(f32)
            stacked = jnp.concatenate(
                [high, scaled - high, jnp.where(iota((32, 128), 0) == 0, 1.0, 0.0)], axis=0
            )
            qaug[b * 128 : (b + 1) * 128] = stacked.T.astype(bf16)

        def block_rows(r, _):
            rows = pl.ds(pl.multiple_of(r * 256, 256), 256)
            scores = jnp.dot(qaug[rows], kaug[...], preferred_element_type=f32) + bf[rows]
            highest = jnp.max(scores, axis=1, keepdims=True)
            probs = jnp.exp2(scores - highest).astype(bf16)
            mixed = lax.dot_general(probs, vaug[...], NT, preferred_element_type=f32).T
            attended = (mixed[0:HW] / mixed[HW : HW + 1]).astype(bf16)
            os_[s, 2 * r] = attended[:, 0:128]
            os_[s, 2 * r + 1] = attended[:, 128:256]
            return 0

        lax.fori_loop(0, 2, block_rows, 0)
        for d in (1, 2, 3):
            o_copy(s, d).start()
        og[s, zh] = os_[s, zh]

    def attention(s, _):
        attend(s)

        @pl.when(s < 2)
        def _():
            forward(s + 2)

        return 0

    lax.fori_loop(0, S, attention, 0)

    for zl_from in range(4):
        for d in (1, 2, 3):
            slot = wog.at[turn(x, -d) * 4 + zl_from]
            remote(slot, slot, pair_of(wo_x, d - 1, zl_from), dev(x=turn(x, -d))).wait_recv()
    wop[...] = jnp.zeros_like(wop)
    for half in range(2):
        blocks = wog[8 * half : 8 * half + 8].astype(f32)
        for side in range(2):
            wop[half, 0:HALF, side * F : (side + 1) * F] = (
                blocks[:, side * 24 : (side + 1) * 24].reshape(HALF, F).astype(bf16)
            )

    def a_copy(s):
        return remote(xs.at[s], at.at[core, s], pair_of(a_c, s), dev(core=other))

    def collect(s, _):
        for d in (1, 2, 3):
            source = turn(zh, -d)
            remote(os_.at[s, 0], og.at[s, source], pair_of(o_zh, s, d - 1), dev(zh=source)).wait_recv()
        stacked = jnp.concatenate([og[s].astype(f32).reshape(HALF, 128), jnp.zeros((64, 128), f32)], axis=0)
        tokens = stacked.T.astype(bf16)
        first, second = tokens[0:T], tokens[T : 2 * T]
        xs[s] = jnp.where(core == 0, second.astype(f32), first.astype(f32)).astype(bf16)
        a_copy(s).start()
        at[core, s] = jnp.where(core == 0, first.astype(f32), second.astype(f32)).astype(bf16)
        return 0

    def finish(s, _):
        slot = at.at[other, s]
        remote(xs.at[s], slot, pair_of(a_c, s), dev(core=other)).wait_recv()
        projected = jnp.dot(at[0, s], wop[0], preferred_element_type=f32) + jnp.dot(
            at[1, s], wop[1], preferred_element_type=f32
        )
        opened = jax.nn.sigmoid(gate[s].astype(f32))
        out[s] = (act[s].astype(f32) + opened * projected).astype(bf16)
        pltpu.make_async_copy(out.at[s], out_h.at[s], out_sem.at[s]).start()
        return 0

    loads[10].wait()
    collect(0, 0)

    def last(s, _):
        collect(s + 1, 0)
        finish(s, 0)
        return 0

    lax.fori_loop(0, S - 1, last, 0)
    finish(S - 1, 0)

    mask_core.wait_send()
    bias_core.wait_send()
    shifted_core.wait_send()
    for copy in (wo_zl_copies + wo_x_copies + b_zh_copies + m_zh_copies + m_y_copies):
        copy.wait_send()

    line_drain(wg, w_zl, w_x)
    line_drain(bg, b_zl, b_x)

    def drain(s, _):
        for d in (1, 2, 3):
            kv_copy(s, d).wait_send()
            q_copy(s, d).wait_send()
            for e in range(4):
                ky_copy(s, d, e).wait_send()
            o_copy(s, d).wait_send()
        a_copy(s).wait_send()
        pltpu.make_async_copy(out.at[s], out_h.at[s], out_sem.at[s]).wait()
        return 0

    lax.fori_loop(0, S, drain, 0)


def body(
    activations, cond_scale, cond_shift, output_gate, pair_repr, bias_weight, query_weight, query_bias, key_weight,
    value_weight, output_weight, token_mask,
):
    vmem = pl.BlockSpec(memory_space=pltpu.VMEM)
    any_ = pl.BlockSpec(memory_space=pl.ANY)
    dma = pltpu.SemaphoreType.DMA
    scratch = [
        *[pltpu.VMEM((S, T, D), bf16)] * 4,
        pltpu.VMEM((T, 128, 128), bf16),
        pltpu.VMEM((8, 128), bf16),
        *[pltpu.VMEM((HW, F), bf16)] * 3,
        pltpu.VMEM((F // 16, D), bf16),
        pltpu.VMEM((S, T), jnp.int32),
        pltpu.VMEM((S, T, D), bf16),
        dma((11,)),
        dma((S,)),
        pltpu.VMEM((16, HW, WC), bf16),
        pltpu.VMEM((16, HW, F), bf16),
        pltpu.VMEM((2, 256, D), bf16),
        pltpu.VMEM((16, WC), f32),
        pltpu.VMEM((S, 2 * T, D), bf16),
        pltpu.VMEM((S, 4, 2 * HW, 128), bf16),
        pltpu.VMEM((S, 4, 4, 2 * HW, 128), bf16),
        pltpu.VMEM((S, 4, HW, 128), bf16),
        pltpu.VMEM((S, 4, HW, 128), bf16),
        pltpu.VMEM((8, T, 128), f32),
        pltpu.VMEM((2, 4, T, 128), bf16),
        pltpu.VMEM((4, 2 * T, 128), bf16),
        pltpu.VMEM((16, 4, 128, 128), bf16),
        pltpu.VMEM((512, KEYS), f32),
        pltpu.VMEM((16, 128), f32),
        pltpu.VMEM((16, 128), bf16),
        pltpu.VMEM((16, 128), bf16),
        pltpu.VMEM((4, 4, 16, 128), bf16),
        pltpu.VMEM((S, 16, KEYS), bf16),
        pltpu.VMEM((128, KEYS), bf16),
        pltpu.VMEM((128, KEYS), bf16),
        pltpu.VMEM((512, 128), bf16),
        pltpu.VMEM((S, 4, HW, 128), bf16),
        pltpu.VMEM((S, 4, HW, 128), bf16),
        pltpu.VMEM((S, T, 256), bf16),
        pltpu.VMEM((2, S, T, 256), bf16),
        dma((2, 2, 4)),
        dma((2, 3, 4)),
        dma((2, 3)),
        dma((2, 3, 4)),
        dma((2, 3)),
        dma((2, 3)),
        dma((2, 2, 4)),
        dma((2, 3, 4)),
        dma((2, 3)),
        dma((2, 3)),
        dma((2, S, 3)),
        dma((2, S, 3)),
        dma((2, S, 3, 4)),
        dma((2, S, 3)),
        dma((2, S)),
    ]
    return pl.pallas_call(
        kernel,
        out_shape=jax.ShapeDtypeStruct((S, T, D), bf16),
        in_specs=[any_] * 7 + [vmem] + [any_] * 4,
        out_specs=any_,
        scratch_shapes=scratch,
        compiler_params=pltpu.CompilerParams(
            collective_id=0, has_side_effects=True, vmem_limit_bytes=56 * 2**20
        ),
        cost_estimate=pl.CostEstimate(flops=2 * 10**9, bytes_accessed=5 * 10**6, transcendentals=4 * 10**6),
        name="pair_attention",
    )(
        activations, cond_scale, cond_shift, output_gate, pair_repr, bias_weight.T, query_weight,
        query_bias, key_weight, value_weight, output_weight, token_mask,
    )


def solution(mesh):
    return jax.shard_map(
        body,
        mesh=mesh,
        in_specs=(
            P("noise", "row", None),
            P("noise", "row", None),
            P("noise", "row", None),
            P("noise", "row", None),
            P("row", "noise", None),
            P(),
            P("noise", None),
            P(),
            P("noise", None),
            P("noise", None),
            P("noise", None),
            P("noise", "row"),
        ),
        out_specs=P("noise", "row", None),
        check_vma=False,
    )
```

```python
import functools
import math

import jax
import jax.numpy as jnp
from jax import lax
from jax.experimental import pallas as pl
from jax.experimental.pallas import tpu as pltpu
from jax.sharding import PartitionSpec as P

MESH = pl.DeviceIdType.MESH
f32 = jnp.float32
bf16 = jnp.bfloat16
epsilon = 1e-05
masked_score = -1e30
LOG2E = math.log2(math.e)

S = 4
T = 64
D = 768
F = 384
HW = 48
HALF = 192
WC = 640
KEYS = 2048
NT = (((1,), (1,)), ((), ()))


def iota(shape, dim):
    return lax.broadcasted_iota(jnp.int32, shape, dim)


def layer_norm(tensor):
    average = jnp.mean(tensor, axis=-1, keepdims=True)
    centred = tensor - average
    variance = jnp.mean(centred * centred, axis=-1, keepdims=True)
    return centred * lax.rsqrt(variance + epsilon)


def kernel(
    act_h, scale_h, shift_h, gate_h, pair_h, wb_h, wq_h, qb_ref, wk_h, wv_h, wo_h, mask_h,
    out_h,
    act, scale, shift, gate, pair, wb_ref, wq_ref, wk_ref, wv_ref, wo_ref, mask_ref, out, local_sem, out_sem,
    wg, wog, wop, qrow,
    sh, kvs, kvg, qs, qg,
    bt, btb, bc, bg, bf,
    mk, mks, mko, mg, mb,
    kaug, vaug, qaug,
    os_, og, xs, at,
    w_zl, w_x, wo_zl, wo_x, c_sem, b_zh, b_zl, b_x, m_zh, m_y, k_zh, q_zh, k_y, o_zh, a_c,
):
    noise, row = lax.axis_index("noise"), lax.axis_index("row")
    x, zl = noise // 4, lax.rem(noise, 4)
    zh, y, core = row // 8, lax.rem(row // 2, 4), lax.rem(row, 2)
    other = 1 - core

    def turn(v, d):
        return lax.rem(v + d + 4, 4)

    def dev(x=x, zl=zl, zh=zh, y=y, core=core):
        return (x * 4 + zl, zh * 8 + y * 2 + core)

    def remote(src, dst, sems, device):
        return pltpu.make_async_remote_copy(
            src_ref=src, dst_ref=dst, send_sem=sems[0], recv_sem=sems[1], device_id=device, device_id_type=MESH
        )

    def pair_of(sem, *index):
        return sem.at[(0, *index)], sem.at[(1, *index)]

    def hop(buffer, sems, way, origin):
        slot = buffer.at[x * 4 + origin]
        return remote(slot, slot, pair_of(sems, way, origin), dev(zl=turn(zl, 1 if way == 0 else -1)))

    def to_x(buffer, sems, origin, d):
        slot = buffer.at[x * 4 + origin]
        return remote(slot, slot, pair_of(sems, d - 1, origin), dev(x=turn(x, d)))

    def pass_on(buffer, z_sems, x_sems, origin, ways):
        for way in ways:

            @pl.when(zl < 3 if way == 0 else zl > 0)
            def _():
                hop(buffer, z_sems, way, origin).start()

        for d in (1, 2, 3):
            to_x(buffer, x_sems, origin, d).start()

    def line_step(buffer, z_sems, x_sems, k):
        @pl.when(zl >= k)
        def _():
            hop(buffer, z_sems, 0, zl - k).wait_recv()
            pass_on(buffer, z_sems, x_sems, zl - k, (0,))

        @pl.when(zl + k <= 3)
        def _():
            hop(buffer, z_sems, 1, zl + k).wait_recv()
            pass_on(buffer, z_sems, x_sems, zl + k, (1,))

    def line_drain(buffer, z_sems, x_sems):
        for origin in range(4):
            for d in (1, 2, 3):
                to_x(buffer, x_sems, origin, d).wait_send()

            @pl.when((zl < 3) & (zl >= origin))
            def _():
                hop(buffer, z_sems, 0, origin).wait_send()

            @pl.when((zl > 0) & (zl <= origin))
            def _():
                hop(buffer, z_sems, 1, origin).wait_send()

    barrier = pltpu.get_barrier_semaphore()
    for d in (1, 2, 3):
        for where in (dev(zh=turn(zh, d)), dev(zl=turn(zl, d)), dev(x=turn(x, d)), dev(y=turn(y, d))):
            pl.semaphore_signal(barrier, inc=1, device_id=where, device_id_type=MESH)
    pl.semaphore_signal(barrier, inc=1, device_id=dev(core=other), device_id_type=MESH)

    loads = [
        pltpu.make_async_copy(source, target, local_sem.at[i])
        for i, (source, target) in enumerate(
            (
                (pair_h, pair), (wb_h, wb_ref), (wq_h, wq_ref), (wk_h, wk_ref), (wv_h, wv_ref), (wo_h, wo_ref),
                (mask_h, mask_ref), (act_h, act), (scale_h, scale), (shift_h, shift), (gate_h, gate),
            )
        )
    ]
    for load in loads:
        load.start()

    for load in loads[2:7]:
        load.wait()

    def chosen(first):
        return ((iota((F, WC), 0) == iota((F, WC), 1) - first + HALF * core)
                & (iota((F, WC), 1) >= first) & (iota((F, WC), 1) < first + HALF)).astype(f32).astype(bf16)

    weights = (
        jnp.dot(wk_ref[...], chosen(0), preferred_element_type=f32)
        + jnp.dot(wv_ref[...], chosen(HALF), preferred_element_type=f32)
        + jnp.dot(wq_ref[...], chosen(2 * HALF), preferred_element_type=f32)
    )
    qrow[...] = jnp.dot(
        jnp.broadcast_to(qb_ref[...].astype(f32).reshape(1, F), (16, F)).astype(bf16), chosen(2 * HALF), preferred_element_type=f32
    )
    wg[noise] = weights.astype(bf16)
    wo = wo_ref[...].astype(f32)
    wog[noise] = jnp.concatenate([wo[:, :F], wo[:, F:]], axis=0).astype(bf16)
    lanes = (iota((T, 128), 1) == iota((T, 128), 0) + T * core).astype(f32).astype(bf16)
    mk[...] = jnp.zeros_like(mk)
    mk[0:S] = jnp.dot(mask_ref[...].astype(f32).astype(bf16), lanes, preferred_element_type=f32)
    mks[...] = mk[...].astype(bf16)

    loads[1].wait()
    wb = jnp.concatenate([wb_ref[...].astype(f32), jnp.zeros((120, 128), f32)], axis=0).T
    wsum = jnp.sum(wb, axis=0, keepdims=True)
    wide = jnp.concatenate([wb, jnp.full((128, 128), 1.0 / 128, f32)], axis=1).astype(bf16)
    mean_at = jnp.where(iota((128, 128), 1) == 8, 1.0 / 128, 0.0).astype(bf16)
    loads[0].wait()

    def pair_rows(step, _):
        tile = pair[pl.ds(step * 8, 8)].reshape(1024, 128)
        both = jnp.dot(tile, wide, preferred_element_type=f32)
        mean = both[:, 128:]
        centred = tile.astype(f32) - mean
        square = (centred * centred).astype(bf16)
        table = both[:, :128] - mean * wsum + jnp.dot(square, mean_at, preferred_element_type=f32)
        for i in range(8):
            flipped = table[i * 128 : (i + 1) * 128].T
            bias = flipped[0:8] * lax.rsqrt(flipped[8:9] + epsilon)
            bt[:, pl.ds(step * 8 + i, 1), :] = bias.reshape(8, 1, 128)
        return 0

    lax.fori_loop(0, 4, pair_rows, 0)

    pl.semaphore_wait(barrier, 13)

    pass_on(wg, w_zl, w_x, zl, (0, 1))
    mask_core = remote(mks, mko, pair_of(c_sem, 0), dev(core=other))
    mask_core.start()

    lax.fori_loop(4, 6, pair_rows, 0)
    line_step(wg, w_zl, w_x, 1)
    lax.fori_loop(6, 8, pair_rows, 0)
    btb[...] = bt[...].astype(bf16).reshape(2, 4, T, 128)
    here = pl.ds(pl.multiple_of(core * T, T), T)
    bias_core = remote(btb.at[other], bc.at[:, here], pair_of(c_sem, 1), dev(core=other))
    bias_core.start()
    bc[:, here] = btb[core]
    line_step(wg, w_zl, w_x, 2)

    there = pl.ds(pl.multiple_of(other * T, T), T)
    remote(btb.at[other], bc.at[:, there], pair_of(c_sem, 1), dev(core=other)).wait_recv()
    b_zh_copies = []
    for d in (1, 2, 3):
        to = turn(zh, d)
        b_zh_copies.append(remote(bc.at[to], bg.at[noise, zh], pair_of(b_zh, d - 1), dev(zh=to)))
        b_zh_copies[-1].start()
    bg[noise, zh] = bc[zh]
    line_step(wg, w_zl, w_x, 3)
    for load in loads[7:10]:
        load.wait()

    def norm_rows(s, _):
        normed = layer_norm(act[s].astype(f32))
        sh[s, here] = (scale[s].astype(f32) * normed + shift[s].astype(f32)).astype(bf16)
        return 0

    lax.fori_loop(0, S, norm_rows, 0)
    shifted_core = remote(sh.at[:, here], sh.at[:, here], pair_of(c_sem, 2), dev(core=other))
    shifted_core.start()

    mask_core.wait_recv()
    mg[y, zh] = mks[...] + mko[...]
    m_zh_copies = []
    for d in (1, 2, 3):
        m_zh_copies.append(remote(mg.at[y, zh], mg.at[y, zh], pair_of(m_zh, d - 1), dev(zh=turn(zh, d))))
        m_zh_copies[-1].start()

    remote(sh.at[:, there], sh.at[:, there], pair_of(c_sem, 2), dev(core=other)).wait_recv()
    for zl_from in range(4):
        for d in (1, 2, 3):
            slot = wg.at[turn(x, -d) * 4 + zl_from]
            remote(slot, slot, pair_of(w_x, d - 1, zl_from), dev(x=turn(x, -d))).wait_recv()

    def kv_copy(s, d):
        to = turn(zh, d)
        return remote(kvs.at[s, to], kvg.at[s, y, zh], pair_of(k_zh, s, d - 1), dev(zh=to))

    def q_copy(s, d):
        to = turn(zh, d)
        return remote(qs.at[s, to], qg.at[s, zh], pair_of(q_zh, s, d - 1), dev(zh=to))

    def ky_copy(s, d, e):
        slot = kvg.at[s, y, turn(zh, -e)]
        return remote(slot, slot, pair_of(k_y, s, d - 1, e), dev(y=turn(y, d)))

    def forward(s):
        for e in (1, 3, 2):
            source = turn(zh, -e)
            remote(kvs.at[s, 0], kvg.at[s, y, source], pair_of(k_zh, s, e - 1), dev(zh=source)).wait_recv()
            for d in (1, 2, 3):
                ky_copy(s, d, e).start()

    def project(s, _):
        rows = jnp.dot(sh[s], wg[...].reshape(D, WC), preferred_element_type=f32) + qrow[0:1]
        flipped = rows.T.astype(bf16)
        for h in range(4):
            kvs[s, h, 0:HW] = flipped[h * HW : (h + 1) * HW]
            kvs[s, h, HW : 2 * HW] = flipped[HALF + h * HW : HALF + (h + 1) * HW]
            qs[s, h] = flipped[2 * HALF + h * HW : 2 * HALF + (h + 1) * HW]
        kvg[s, y, zh] = kvs[s, zh]
        qg[s, zh] = qs[s, zh]
        return 0

    def exchange(s, _):
        for d in (1, 2, 3):
            kv_copy(s, d).start()
        for d in (1, 2, 3):
            ky_copy(s, d, 0).start()
        return 0

    def exchange_q(s):
        for d in (1, 2, 3):
            q_copy(s, d).start()

    project(0, 0)
    exchange(0, 0)

    for d in (1, 2, 3):
        source = turn(zh, -d)
        remote(bc.at[0], bg.at[noise, source], pair_of(b_zh, d - 1), dev(zh=source)).wait_recv()
    pass_on(bg, b_zl, b_x, zl, (0, 1))
    lax.fori_loop(1, S, project, 0)
    line_step(bg, b_zl, b_x, 1)
    exchange(1, 0)
    exchange_q(0)
    for k in (2, 3):
        line_step(bg, b_zl, b_x, k)
    wo_zl_copies = [
        remote(wog.at[noise], wog.at[noise], pair_of(wo_zl, d - 1), dev(zl=turn(zl, d))) for d in (1, 2, 3)
    ]
    for copy in wo_zl_copies:
        copy.start()
    for d in (1, 2, 3):
        source = turn(zh, -d)
        slot = mg.at[y, source]
        remote(slot, slot, pair_of(m_zh, d - 1), dev(zh=source)).wait_recv()
    m_y_copies = []
    for d in (1, 2, 3):
        m_y_copies.append(remote(mg.at[y], mg.at[y], pair_of(m_y, d - 1), dev(y=turn(y, d))))
        m_y_copies[-1].start()


    def wo_x_send(zl_from):
        block = x * 4 + zl_from
        copies = []
        for d in (1, 2, 3):
            copies.append(remote(wog.at[block], wog.at[block], pair_of(wo_x, d - 1, zl_from), dev(x=turn(x, d))))
            copies[-1].start()
        return copies

    forward(0)
    exchange(2, 0)
    exchange_q(1)
    wo_x_copies = wo_x_send(zl)
    for d in (1, 2, 3):
        source = turn(zl, -d)
        slot = wog.at[x * 4 + source]
        remote(slot, slot, pair_of(wo_zl, d - 1), dev(zl=source)).wait_recv()
        wo_x_copies += wo_x_send(source)

    for d in (1, 2, 3):
        source = turn(y, -d)
        remote(mg.at[source], mg.at[source], pair_of(m_y, d - 1), dev(y=source)).wait_recv()
    for b in range(16):
        tokens = mg[b % 4, b // 4].astype(f32)
        for s in range(S):
            line = (tokens[s : s + 1] - 1.0) * (-masked_score)
            mb[s, :, b * 128 : (b + 1) * 128] = jnp.where(
                iota((16, 128), 0) == 0, jnp.broadcast_to(line, (16, 128)), 0.0
            ).astype(bf16)
    kaug[112:128] = jnp.zeros((16, KEYS), bf16)
    vaug[HW:128] = jnp.where(iota((80, KEYS), 0) == 0, 1.0, 0.0).astype(bf16)

    forward(1)
    exchange(3, 0)
    exchange_q(2)
    exchange_q(3)

    for zl_from in range(4):
        for d in (1, 2, 3):
            slot = bg.at[turn(x, -d) * 4 + zl_from]
            remote(slot, slot, pair_of(b_x, d - 1, zl_from), dev(x=turn(x, -d))).wait_recv()

    def widen(b, _):
        columns = pl.ds(pl.multiple_of(b * 128, 128), 128)
        bf[:, columns] = bg[b].reshape(512, 128).astype(f32) * LOG2E
        return 0

    lax.fori_loop(0, 16, widen, 0)

    def o_copy(s, d):
        to = turn(zh, d)
        return remote(os_.at[s, to], og.at[s, zh], pair_of(o_zh, s, d - 1), dev(zh=to))

    def attend(s):
        for d in (1, 2, 3):
            source = turn(zh, -d)
            remote(qs.at[s, 0], qg.at[s, source], pair_of(q_zh, s, d - 1), dev(zh=source)).wait_recv()
        for d in (1, 2, 3):
            source = turn(y, -d)
            for e in range(4):
                slot = kvg.at[s, source, turn(zh, -e)]
                remote(slot, slot, pair_of(k_y, s, d - 1, e), dev(y=source)).wait_recv()
        for b in range(16):
            columns = slice(b * 128, (b + 1) * 128)
            block = kvg[s, b % 4, b // 4]
            kaug[0:HW, columns] = block[0:HW]
            kaug[HW : 2 * HW, columns] = block[0:HW]
            vaug[0:HW, columns] = block[HW : 2 * HW]
        kaug[96:112] = mb[s]
        for b in range(4):
            scaled = qg[s, b].astype(f32) * (LOG2E / math.sqrt(HW))
            high = scaled.astype(bf16).astype(f32)
            stacked = jnp.concatenate(
                [high, scaled - high, jnp.where(iota((32, 128), 0) == 0, 1.0, 0.0)], axis=0
            )
            qaug[b * 128 : (b + 1) * 128] = stacked.T.astype(bf16)

        def block_rows(r, _):
            rows = slice(0, 512)
            scores = jnp.dot(qaug[rows], kaug[...], preferred_element_type=f32) + bf[rows]
            highest = jnp.max(scores, axis=1, keepdims=True)
            probs = jnp.exp2(scores - highest).astype(bf16)
            mixed = lax.dot_general(probs, vaug[...], NT, preferred_element_type=f32).T
            attended = (mixed[0:HW] / mixed[HW : HW + 1]).astype(bf16)
            for b in range(4):
                os_[s, b] = attended[:, b * 128 : (b + 1) * 128]
            return 0

        block_rows(0, 0)
        for d in (1, 2, 3):
            o_copy(s, d).start()
        og[s, zh] = os_[s, zh]

    def attention(s, _):
        attend(s)

        @pl.when(s < 2)
        def _():
            forward(s + 2)

        return 0

    lax.fori_loop(0, S, attention, 0)

    for zl_from in range(4):
        for d in (1, 2, 3):
            slot = wog.at[turn(x, -d) * 4 + zl_from]
            remote(slot, slot, pair_of(wo_x, d - 1, zl_from), dev(x=turn(x, -d))).wait_recv()
    wop[...] = jnp.zeros_like(wop)
    for half in range(2):
        blocks = wog[8 * half : 8 * half + 8].astype(f32)
        for side in range(2):
            wop[half, 0:HALF, side * F : (side + 1) * F] = (
                blocks[:, side * 24 : (side + 1) * 24].reshape(HALF, F).astype(bf16)
            )

    def a_copy(s):
        return remote(xs.at[s], at.at[core, s], pair_of(a_c, s), dev(core=other))

    def collect(s, _):
        for d in (1, 2, 3):
            source = turn(zh, -d)
            remote(os_.at[s, 0], og.at[s, source], pair_of(o_zh, s, d - 1), dev(zh=source)).wait_recv()
        stacked = jnp.concatenate([og[s].astype(f32).reshape(HALF, 128), jnp.zeros((64, 128), f32)], axis=0)
        tokens = stacked.T.astype(bf16)
        first, second = tokens[0:T], tokens[T : 2 * T]
        xs[s] = jnp.where(core == 0, second.astype(f32), first.astype(f32)).astype(bf16)
        a_copy(s).start()
        at[core, s] = jnp.where(core == 0, first.astype(f32), second.astype(f32)).astype(bf16)
        return 0

    def finish(s, _):
        slot = at.at[other, s]
        remote(xs.at[s], slot, pair_of(a_c, s), dev(core=other)).wait_recv()
        projected = jnp.dot(at[0, s], wop[0], preferred_element_type=f32) + jnp.dot(
            at[1, s], wop[1], preferred_element_type=f32
        )
        opened = jax.nn.sigmoid(gate[s].astype(f32))
        out[s] = (act[s].astype(f32) + opened * projected).astype(bf16)
        pltpu.make_async_copy(out.at[s], out_h.at[s], out_sem.at[s]).start()
        return 0

    loads[10].wait()
    collect(0, 0)

    def last(s, _):
        collect(s + 1, 0)
        finish(s, 0)
        return 0

    lax.fori_loop(0, S - 1, last, 0)
    finish(S - 1, 0)

    mask_core.wait_send()
    bias_core.wait_send()
    shifted_core.wait_send()
    for copy in (wo_zl_copies + wo_x_copies + b_zh_copies + m_zh_copies + m_y_copies):
        copy.wait_send()

    line_drain(wg, w_zl, w_x)
    line_drain(bg, b_zl, b_x)

    def drain(s, _):
        for d in (1, 2, 3):
            kv_copy(s, d).wait_send()
            q_copy(s, d).wait_send()
            for e in range(4):
                ky_copy(s, d, e).wait_send()
            o_copy(s, d).wait_send()
        a_copy(s).wait_send()
        pltpu.make_async_copy(out.at[s], out_h.at[s], out_sem.at[s]).wait()
        return 0

    lax.fori_loop(0, S, drain, 0)


def body(
    activations, cond_scale, cond_shift, output_gate, pair_repr, bias_weight, query_weight, query_bias, key_weight,
    value_weight, output_weight, token_mask,
):
    vmem = pl.BlockSpec(memory_space=pltpu.VMEM)
    any_ = pl.BlockSpec(memory_space=pl.ANY)
    dma = pltpu.SemaphoreType.DMA
    scratch = [
        *[pltpu.VMEM((S, T, D), bf16)] * 4,
        pltpu.VMEM((T, 128, 128), bf16),
        pltpu.VMEM((8, 128), bf16),
        *[pltpu.VMEM((HW, F), bf16)] * 3,
        pltpu.VMEM((F // 16, D), bf16),
        pltpu.VMEM((S, T), jnp.int32),
        pltpu.VMEM((S, T, D), bf16),
        dma((11,)),
        dma((S,)),
        pltpu.VMEM((16, HW, WC), bf16),
        pltpu.VMEM((16, HW, F), bf16),
        pltpu.VMEM((2, 256, D), bf16),
        pltpu.VMEM((16, WC), f32),
        pltpu.VMEM((S, 2 * T, D), bf16),
        pltpu.VMEM((S, 4, 2 * HW, 128), bf16),
        pltpu.VMEM((S, 4, 4, 2 * HW, 128), bf16),
        pltpu.VMEM((S, 4, HW, 128), bf16),
        pltpu.VMEM((S, 4, HW, 128), bf16),
        pltpu.VMEM((8, T, 128), f32),
        pltpu.VMEM((2, 4, T, 128), bf16),
        pltpu.VMEM((4, 2 * T, 128), bf16),
        pltpu.VMEM((16, 4, 128, 128), bf16),
        pltpu.VMEM((512, KEYS), f32),
        pltpu.VMEM((16, 128), f32),
        pltpu.VMEM((16, 128), bf16),
        pltpu.VMEM((16, 128), bf16),
        pltpu.VMEM((4, 4, 16, 128), bf16),
        pltpu.VMEM((S, 16, KEYS), bf16),
        pltpu.VMEM((128, KEYS), bf16),
        pltpu.VMEM((128, KEYS), bf16),
        pltpu.VMEM((512, 128), bf16),
        pltpu.VMEM((S, 4, HW, 128), bf16),
        pltpu.VMEM((S, 4, HW, 128), bf16),
        pltpu.VMEM((S, T, 256), bf16),
        pltpu.VMEM((2, S, T, 256), bf16),
        dma((2, 2, 4)),
        dma((2, 3, 4)),
        dma((2, 3)),
        dma((2, 3, 4)),
        dma((2, 3)),
        dma((2, 3)),
        dma((2, 2, 4)),
        dma((2, 3, 4)),
        dma((2, 3)),
        dma((2, 3)),
        dma((2, S, 3)),
        dma((2, S, 3)),
        dma((2, S, 3, 4)),
        dma((2, S, 3)),
        dma((2, S)),
    ]
    return pl.pallas_call(
        kernel,
        out_shape=jax.ShapeDtypeStruct((S, T, D), bf16),
        in_specs=[any_] * 7 + [vmem] + [any_] * 4,
        out_specs=any_,
        scratch_shapes=scratch,
        compiler_params=pltpu.CompilerParams(
            collective_id=0, has_side_effects=True, vmem_limit_bytes=56 * 2**20
        ),
        cost_estimate=pl.CostEstimate(flops=2 * 10**9, bytes_accessed=5 * 10**6, transcendentals=4 * 10**6),
        name="pair_attention",
    )(
        activations, cond_scale, cond_shift, output_gate, pair_repr, bias_weight.T, query_weight,
        query_bias, key_weight, value_weight, output_weight, token_mask,
    )


def solution(mesh):
    return jax.shard_map(
        body,
        mesh=mesh,
        in_specs=(
            P("noise", "row", None),
            P("noise", "row", None),
            P("noise", "row", None),
            P("noise", "row", None),
            P("row", "noise", None),
            P(),
            P("noise", None),
            P(),
            P("noise", None),
            P("noise", None),
            P("noise", None),
            P("noise", "row"),
        ),
        out_specs=P("noise", "row", None),
        check_vma=False,
    )
```

```python
import functools
import math

import jax
import jax.numpy as jnp
from jax import lax
from jax.experimental import pallas as pl
from jax.experimental.pallas import tpu as pltpu
from jax.sharding import PartitionSpec as P

MESH = pl.DeviceIdType.MESH
f32 = jnp.float32
bf16 = jnp.bfloat16
epsilon = 1e-05
masked_score = -1e30
LOG2E = math.log2(math.e)

S = 4
T = 64
D = 768
F = 384
HW = 48
HALF = 192
WC = 640
KEYS = 2048
NT = (((1,), (1,)), ((), ()))


def iota(shape, dim):
    return lax.broadcasted_iota(jnp.int32, shape, dim)


def layer_norm(tensor):
    average = jnp.mean(tensor, axis=-1, keepdims=True)
    centred = tensor - average
    variance = jnp.mean(centred * centred, axis=-1, keepdims=True)
    return centred * lax.rsqrt(variance + epsilon)


def kernel(
    act_h, scale_h, shift_h, gate_h, pair_h, wb_h, wq_h, qb_ref, wk_h, wv_h, wo_h, mask_h,
    out_h,
    act, scale, shift, gate, pair, wb_ref, wq_ref, wk_ref, wv_ref, wo_ref, mask_ref, out, local_sem, out_sem,
    wg, wog, wop, qrow,
    sh, kvs, kvg, qs, qg,
    bt, btb, bc, bg, bf,
    mk, mks, mko, mg, mb,
    kaug, vaug, qaug,
    os_, og, xs, at,
    w_zl, w_x, wo_zl, wo_x, c_sem, b_zh, b_zl, b_x, m_zh, m_y, k_zh, q_zh, k_y, o_zh, a_c,
):
    noise, row = lax.axis_index("noise"), lax.axis_index("row")
    x, zl = noise // 4, lax.rem(noise, 4)
    zh, y, core = row // 8, lax.rem(row // 2, 4), lax.rem(row, 2)
    other = 1 - core

    def turn(v, d):
        return lax.rem(v + d + 4, 4)

    def dev(x=x, zl=zl, zh=zh, y=y, core=core):
        return (x * 4 + zl, zh * 8 + y * 2 + core)

    def remote(src, dst, sems, device):
        return pltpu.make_async_remote_copy(
            src_ref=src, dst_ref=dst, send_sem=sems[0], recv_sem=sems[1], device_id=device, device_id_type=MESH
        )

    def pair_of(sem, *index):
        return sem.at[(0, *index)], sem.at[(1, *index)]

    def hop(buffer, sems, way, origin):
        slot = buffer.at[x * 4 + origin]
        return remote(slot, slot, pair_of(sems, way, origin), dev(zl=turn(zl, 1 if way == 0 else -1)))

    def to_x(buffer, sems, origin, d):
        slot = buffer.at[x * 4 + origin]
        return remote(slot, slot, pair_of(sems, d - 1, origin), dev(x=turn(x, d)))

    def pass_on(buffer, z_sems, x_sems, origin, ways):
        for way in ways:

            @pl.when(zl < 3 if way == 0 else zl > 0)
            def _():
                hop(buffer, z_sems, way, origin).start()

        for d in (1, 2, 3):
            to_x(buffer, x_sems, origin, d).start()

    def line_step(buffer, z_sems, x_sems, k):
        @pl.when(zl >= k)
        def _():
            hop(buffer, z_sems, 0, zl - k).wait_recv()
            pass_on(buffer, z_sems, x_sems, zl - k, (0,))

        @pl.when(zl + k <= 3)
        def _():
            hop(buffer, z_sems, 1, zl + k).wait_recv()
            pass_on(buffer, z_sems, x_sems, zl + k, (1,))

    def line_drain(buffer, z_sems, x_sems):
        for origin in range(4):
            for d in (1, 2, 3):
                to_x(buffer, x_sems, origin, d).wait_send()

            @pl.when((zl < 3) & (zl >= origin))
            def _():
                hop(buffer, z_sems, 0, origin).wait_send()

            @pl.when((zl > 0) & (zl <= origin))
            def _():
                hop(buffer, z_sems, 1, origin).wait_send()

    barrier = pltpu.get_barrier_semaphore()
    for d in (1, 2, 3):
        for where in (dev(zh=turn(zh, d)), dev(zl=turn(zl, d)), dev(x=turn(x, d)), dev(y=turn(y, d))):
            pl.semaphore_signal(barrier, inc=1, device_id=where, device_id_type=MESH)
    pl.semaphore_signal(barrier, inc=1, device_id=dev(core=other), device_id_type=MESH)

    loads = [
        pltpu.make_async_copy(source, target, local_sem.at[i])
        for i, (source, target) in enumerate(
            (
                (pair_h, pair), (wb_h, wb_ref), (wq_h, wq_ref), (wk_h, wk_ref), (wv_h, wv_ref), (wo_h, wo_ref),
                (mask_h, mask_ref), (act_h, act), (scale_h, scale), (shift_h, shift), (gate_h, gate),
            )
        )
    ]
    for load in loads:
        load.start()

    for load in loads[2:7]:
        load.wait()

    def chosen(first):
        return ((iota((F, WC), 0) == iota((F, WC), 1) - first + HALF * core)
                & (iota((F, WC), 1) >= first) & (iota((F, WC), 1) < first + HALF)).astype(f32).astype(bf16)

    weights = (
        jnp.dot(wk_ref[...], chosen(0), preferred_element_type=f32)
        + jnp.dot(wv_ref[...], chosen(HALF), preferred_element_type=f32)
        + jnp.dot(wq_ref[...], chosen(2 * HALF), preferred_element_type=f32)
    )
    qrow[...] = jnp.dot(
        jnp.broadcast_to(qb_ref[...].astype(f32).reshape(1, F), (16, F)).astype(bf16), chosen(2 * HALF), preferred_element_type=f32
    )
    wg[noise] = weights.astype(bf16)
    wo = wo_ref[...].astype(f32)
    wog[noise] = jnp.concatenate([wo[:, :F], wo[:, F:]], axis=0).astype(bf16)
    lanes = (iota((T, 128), 1) == iota((T, 128), 0) + T * core).astype(f32).astype(bf16)
    mk[...] = jnp.zeros_like(mk)
    mk[0:S] = jnp.dot(mask_ref[...].astype(f32).astype(bf16), lanes, preferred_element_type=f32)
    mks[...] = mk[...].astype(bf16)

    loads[1].wait()
    wb = wb_ref[...].astype(f32)
    wsum = jnp.sum(wb, axis=1, keepdims=True)
    wide = jnp.concatenate([wb, jnp.full((8, 128), 1.0 / 128, f32)], axis=0).astype(bf16)
    evens = jnp.full((128, 128), 1.0 / 128, f32).astype(bf16)
    loads[0].wait()

    def pair_rows(step, _):
        tile = pair[pl.ds(step * 8, 8)].reshape(1024, 128)
        centred = tile.astype(f32) - jnp.dot(tile, evens, preferred_element_type=f32)
        square = (centred * centred).astype(bf16)
        table = lax.dot_general(wide, tile, NT, preferred_element_type=f32)
        variance = lax.dot_general(evens[0:16], square, NT, preferred_element_type=f32)
        biases = (table[0:8] - table[8:9] * wsum) * lax.rsqrt(variance[0:8] + epsilon)
        for i in range(8):
            bias = biases[:, i * 128 : (i + 1) * 128]
            bt[:, pl.ds(step * 8 + i, 1), :] = bias.reshape(8, 1, 128)
        return 0

    lax.fori_loop(0, 6, pair_rows, 0)

    pl.semaphore_wait(barrier, 13)

    pass_on(wg, w_zl, w_x, zl, (0, 1))
    mask_core = remote(mks, mko, pair_of(c_sem, 0), dev(core=other))
    mask_core.start()

    lax.fori_loop(6, 7, pair_rows, 0)
    line_step(wg, w_zl, w_x, 1)
    lax.fori_loop(7, 8, pair_rows, 0)
    btb[...] = bt[...].astype(bf16).reshape(2, 4, T, 128)
    here = pl.ds(pl.multiple_of(core * T, T), T)
    bias_core = remote(btb.at[other], bc.at[:, here], pair_of(c_sem, 1), dev(core=other))
    bias_core.start()
    bc[:, here] = btb[core]
    line_step(wg, w_zl, w_x, 2)

    there = pl.ds(pl.multiple_of(other * T, T), T)
    remote(btb.at[other], bc.at[:, there], pair_of(c_sem, 1), dev(core=other)).wait_recv()
    b_zh_copies = []
    for d in (1, 2, 3):
        to = turn(zh, d)
        b_zh_copies.append(remote(bc.at[to], bg.at[noise, zh], pair_of(b_zh, d - 1), dev(zh=to)))
        b_zh_copies[-1].start()
    bg[noise, zh] = bc[zh]
    line_step(wg, w_zl, w_x, 3)
    for load in loads[7:10]:
        load.wait()

    def norm_rows(s, _):
        normed = layer_norm(act[s].astype(f32))
        sh[s, here] = (scale[s].astype(f32) * normed + shift[s].astype(f32)).astype(bf16)
        return 0

    lax.fori_loop(0, S, norm_rows, 0)
    shifted_core = remote(sh.at[:, here], sh.at[:, here], pair_of(c_sem, 2), dev(core=other))
    shifted_core.start()

    mask_core.wait_recv()
    mg[y, zh] = mks[...] + mko[...]
    m_zh_copies = []
    for d in (1, 2, 3):
        m_zh_copies.append(remote(mg.at[y, zh], mg.at[y, zh], pair_of(m_zh, d - 1), dev(zh=turn(zh, d))))
        m_zh_copies[-1].start()

    remote(sh.at[:, there], sh.at[:, there], pair_of(c_sem, 2), dev(core=other)).wait_recv()
    for zl_from in range(4):
        for d in (1, 2, 3):
            slot = wg.at[turn(x, -d) * 4 + zl_from]
            remote(slot, slot, pair_of(w_x, d - 1, zl_from), dev(x=turn(x, -d))).wait_recv()

    def kv_copy(s, d):
        to = turn(zh, d)
        return remote(kvs.at[s, to], kvg.at[s, y, zh], pair_of(k_zh, s, d - 1), dev(zh=to))

    def q_copy(s, d):
        to = turn(zh, d)
        return remote(qs.at[s, to], qg.at[s, zh], pair_of(q_zh, s, d - 1), dev(zh=to))

    def ky_copy(s, d, e):
        slot = kvg.at[s, y, turn(zh, -e)]
        return remote(slot, slot, pair_of(k_y, s, d - 1, e), dev(y=turn(y, d)))

    def forward(s):
        for e in (1, 3, 2):
            source = turn(zh, -e)
            remote(kvs.at[s, 0], kvg.at[s, y, source], pair_of(k_zh, s, e - 1), dev(zh=source)).wait_recv()
            for d in (1, 2, 3):
                ky_copy(s, d, e).start()

    def project(s, _):
        rows = jnp.dot(sh[s], wg[...].reshape(D, WC), preferred_element_type=f32) + qrow[0:1]
        flipped = rows.T.astype(bf16)
        for h in range(4):
            kvs[s, h, 0:HW] = flipped[h * HW : (h + 1) * HW]
            kvs[s, h, HW : 2 * HW] = flipped[HALF + h * HW : HALF + (h + 1) * HW]
            qs[s, h] = flipped[2 * HALF + h * HW : 2 * HALF + (h + 1) * HW]
        kvg[s, y, zh] = kvs[s, zh]
        qg[s, zh] = qs[s, zh]
        return 0

    def exchange(s, _):
        for d in (1, 2, 3):
            kv_copy(s, d).start()
        for d in (1, 2, 3):
            ky_copy(s, d, 0).start()
        return 0

    def exchange_q(s):
        for d in (1, 2, 3):
            q_copy(s, d).start()

    project(0, 0)
    exchange(0, 0)

    for d in (1, 2, 3):
        source = turn(zh, -d)
        remote(bc.at[0], bg.at[noise, source], pair_of(b_zh, d - 1), dev(zh=source)).wait_recv()
    pass_on(bg, b_zl, b_x, zl, (0, 1))
    lax.fori_loop(1, S, project, 0)
    line_step(bg, b_zl, b_x, 1)
    exchange(1, 0)
    exchange_q(0)
    for k in (2, 3):
        line_step(bg, b_zl, b_x, k)
    wo_zl_copies = [
        remote(wog.at[noise], wog.at[noise], pair_of(wo_zl, d - 1), dev(zl=turn(zl, d))) for d in (1, 2, 3)
    ]
    for copy in wo_zl_copies:
        copy.start()
    for d in (1, 2, 3):
        source = turn(zh, -d)
        slot = mg.at[y, source]
        remote(slot, slot, pair_of(m_zh, d - 1), dev(zh=source)).wait_recv()
    m_y_copies = []
    for d in (1, 2, 3):
        m_y_copies.append(remote(mg.at[y], mg.at[y], pair_of(m_y, d - 1), dev(y=turn(y, d))))
        m_y_copies[-1].start()


    def wo_x_send(zl_from):
        block = x * 4 + zl_from
        copies = []
        for d in (1, 2, 3):
            copies.append(remote(wog.at[block], wog.at[block], pair_of(wo_x, d - 1, zl_from), dev(x=turn(x, d))))
            copies[-1].start()
        return copies

    forward(0)
    exchange(2, 0)
    exchange_q(1)
    wo_x_copies = wo_x_send(zl)
    for d in (1, 2, 3):
        source = turn(zl, -d)
        slot = wog.at[x * 4 + source]
        remote(slot, slot, pair_of(wo_zl, d - 1), dev(zl=source)).wait_recv()
        wo_x_copies += wo_x_send(source)

    for d in (1, 2, 3):
        source = turn(y, -d)
        remote(mg.at[source], mg.at[source], pair_of(m_y, d - 1), dev(y=source)).wait_recv()
    for b in range(16):
        tokens = mg[b % 4, b // 4].astype(f32)
        for s in range(S):
            line = (tokens[s : s + 1] - 1.0) * (-masked_score)
            mb[s, :, b * 128 : (b + 1) * 128] = jnp.where(
                iota((16, 128), 0) == 0, jnp.broadcast_to(line, (16, 128)), 0.0
            ).astype(bf16)
    kaug[112:128] = jnp.zeros((16, KEYS), bf16)
    vaug[HW:128] = jnp.where(iota((80, KEYS), 0) == 0, 1.0, 0.0).astype(bf16)

    forward(1)
    exchange(3, 0)
    exchange_q(2)
    exchange_q(3)

    for zl_from in range(4):
        for d in (1, 2, 3):
            slot = bg.at[turn(x, -d) * 4 + zl_from]
            remote(slot, slot, pair_of(b_x, d - 1, zl_from), dev(x=turn(x, -d))).wait_recv()

    def widen(b, _):
        columns = pl.ds(pl.multiple_of(b * 128, 128), 128)
        bf[:, columns] = bg[b].reshape(512, 128).astype(f32) * LOG2E
        return 0

    lax.fori_loop(0, 16, widen, 0)

    def o_copy(s, d):
        to = turn(zh, d)
        return remote(os_.at[s, to], og.at[s, zh], pair_of(o_zh, s, d - 1), dev(zh=to))

    def attend(s):
        for d in (1, 2, 3):
            source = turn(zh, -d)
            remote(qs.at[s, 0], qg.at[s, source], pair_of(q_zh, s, d - 1), dev(zh=source)).wait_recv()
        for d in (1, 2, 3):
            source = turn(y, -d)
            for e in range(4):
                slot = kvg.at[s, source, turn(zh, -e)]
                remote(slot, slot, pair_of(k_y, s, d - 1, e), dev(y=source)).wait_recv()
        for b in range(16):
            columns = slice(b * 128, (b + 1) * 128)
            block = kvg[s, b % 4, b // 4]
            kaug[0:HW, columns] = block[0:HW]
            kaug[HW : 2 * HW, columns] = block[0:HW]
            vaug[0:HW, columns] = block[HW : 2 * HW]
        kaug[96:112] = mb[s]
        for b in range(4):
            scaled = qg[s, b].astype(f32) * (LOG2E / math.sqrt(HW))
            high = scaled.astype(bf16).astype(f32)
            stacked = jnp.concatenate(
                [high, scaled - high, jnp.where(iota((32, 128), 0) == 0, 1.0, 0.0)], axis=0
            )
            qaug[b * 128 : (b + 1) * 128] = stacked.T.astype(bf16)

        def block_rows(r, _):
            rows = slice(0, 512)
            scores = jnp.dot(qaug[rows], kaug[...], preferred_element_type=f32) + bf[rows]
            highest = jnp.max(scores, axis=1, keepdims=True)
            probs = jnp.exp2(scores - highest).astype(bf16)
            mixed = lax.dot_general(probs, vaug[...], NT, preferred_element_type=f32).T
            attended = (mixed[0:HW] / mixed[HW : HW + 1]).astype(bf16)
            for b in range(4):
                os_[s, b] = attended[:, b * 128 : (b + 1) * 128]
            return 0

        block_rows(0, 0)
        for d in (1, 2, 3):
            o_copy(s, d).start()
        og[s, zh] = os_[s, zh]

    def attention(s, _):
        attend(s)

        @pl.when(s < 2)
        def _():
            forward(s + 2)

        return 0

    lax.fori_loop(0, S, attention, 0)

    for zl_from in range(4):
        for d in (1, 2, 3):
            slot = wog.at[turn(x, -d) * 4 + zl_from]
            remote(slot, slot, pair_of(wo_x, d - 1, zl_from), dev(x=turn(x, -d))).wait_recv()
    wop[...] = jnp.zeros_like(wop)
    for half in range(2):
        blocks = wog[8 * half : 8 * half + 8].astype(f32)
        for side in range(2):
            wop[half, 0:HALF, side * F : (side + 1) * F] = (
                blocks[:, side * 24 : (side + 1) * 24].reshape(HALF, F).astype(bf16)
            )

    def a_copy(s):
        return remote(xs.at[s], at.at[core, s], pair_of(a_c, s), dev(core=other))

    def collect(s, _):
        for d in (1, 2, 3):
            source = turn(zh, -d)
            remote(os_.at[s, 0], og.at[s, source], pair_of(o_zh, s, d - 1), dev(zh=source)).wait_recv()
        stacked = jnp.concatenate([og[s].astype(f32).reshape(HALF, 128), jnp.zeros((64, 128), f32)], axis=0)
        tokens = stacked.T.astype(bf16)
        first, second = tokens[0:T], tokens[T : 2 * T]
        xs[s] = jnp.where(core == 0, second.astype(f32), first.astype(f32)).astype(bf16)
        a_copy(s).start()
        at[core, s] = jnp.where(core == 0, first.astype(f32), second.astype(f32)).astype(bf16)
        return 0

    def finish(s, _):
        slot = at.at[other, s]
        remote(xs.at[s], slot, pair_of(a_c, s), dev(core=other)).wait_recv()
        projected = jnp.dot(at[0, s], wop[0], preferred_element_type=f32) + jnp.dot(
            at[1, s], wop[1], preferred_element_type=f32
        )
        opened = jax.nn.sigmoid(gate[s].astype(f32))
        out[s] = (act[s].astype(f32) + opened * projected).astype(bf16)
        pltpu.make_async_copy(out.at[s], out_h.at[s], out_sem.at[s]).start()
        return 0

    loads[10].wait()
    collect(0, 0)

    def last(s, _):
        collect(s + 1, 0)
        finish(s, 0)
        return 0

    lax.fori_loop(0, S - 1, last, 0)
    finish(S - 1, 0)

    mask_core.wait_send()
    bias_core.wait_send()
    shifted_core.wait_send()
    for copy in (wo_zl_copies + wo_x_copies + b_zh_copies + m_zh_copies + m_y_copies):
        copy.wait_send()

    line_drain(wg, w_zl, w_x)
    line_drain(bg, b_zl, b_x)

    def drain(s, _):
        for d in (1, 2, 3):
            kv_copy(s, d).wait_send()
            q_copy(s, d).wait_send()
            for e in range(4):
                ky_copy(s, d, e).wait_send()
            o_copy(s, d).wait_send()
        a_copy(s).wait_send()
        pltpu.make_async_copy(out.at[s], out_h.at[s], out_sem.at[s]).wait()
        return 0

    lax.fori_loop(0, S, drain, 0)


def body(
    activations, cond_scale, cond_shift, output_gate, pair_repr, bias_weight, query_weight, query_bias, key_weight,
    value_weight, output_weight, token_mask,
):
    vmem = pl.BlockSpec(memory_space=pltpu.VMEM)
    any_ = pl.BlockSpec(memory_space=pl.ANY)
    dma = pltpu.SemaphoreType.DMA
    scratch = [
        *[pltpu.VMEM((S, T, D), bf16)] * 4,
        pltpu.VMEM((T, 128, 128), bf16),
        pltpu.VMEM((8, 128), bf16),
        *[pltpu.VMEM((HW, F), bf16)] * 3,
        pltpu.VMEM((F // 16, D), bf16),
        pltpu.VMEM((S, T), jnp.int32),
        pltpu.VMEM((S, T, D), bf16),
        dma((11,)),
        dma((S,)),
        pltpu.VMEM((16, HW, WC), bf16),
        pltpu.VMEM((16, HW, F), bf16),
        pltpu.VMEM((2, 256, D), bf16),
        pltpu.VMEM((16, WC), f32),
        pltpu.VMEM((S, 2 * T, D), bf16),
        pltpu.VMEM((S, 4, 2 * HW, 128), bf16),
        pltpu.VMEM((S, 4, 4, 2 * HW, 128), bf16),
        pltpu.VMEM((S, 4, HW, 128), bf16),
        pltpu.VMEM((S, 4, HW, 128), bf16),
        pltpu.VMEM((8, T, 128), f32),
        pltpu.VMEM((2, 4, T, 128), bf16),
        pltpu.VMEM((4, 2 * T, 128), bf16),
        pltpu.VMEM((16, 4, 128, 128), bf16),
        pltpu.VMEM((512, KEYS), f32),
        pltpu.VMEM((16, 128), f32),
        pltpu.VMEM((16, 128), bf16),
        pltpu.VMEM((16, 128), bf16),
        pltpu.VMEM((4, 4, 16, 128), bf16),
        pltpu.VMEM((S, 16, KEYS), bf16),
        pltpu.VMEM((128, KEYS), bf16),
        pltpu.VMEM((128, KEYS), bf16),
        pltpu.VMEM((512, 128), bf16),
        pltpu.VMEM((S, 4, HW, 128), bf16),
        pltpu.VMEM((S, 4, HW, 128), bf16),
        pltpu.VMEM((S, T, 256), bf16),
        pltpu.VMEM((2, S, T, 256), bf16),
        dma((2, 2, 4)),
        dma((2, 3, 4)),
        dma((2, 3)),
        dma((2, 3, 4)),
        dma((2, 3)),
        dma((2, 3)),
        dma((2, 2, 4)),
        dma((2, 3, 4)),
        dma((2, 3)),
        dma((2, 3)),
        dma((2, S, 3)),
        dma((2, S, 3)),
        dma((2, S, 3, 4)),
        dma((2, S, 3)),
        dma((2, S)),
    ]
    return pl.pallas_call(
        kernel,
        out_shape=jax.ShapeDtypeStruct((S, T, D), bf16),
        in_specs=[any_] * 7 + [vmem] + [any_] * 4,
        out_specs=any_,
        scratch_shapes=scratch,
        compiler_params=pltpu.CompilerParams(
            collective_id=0, has_side_effects=True, vmem_limit_bytes=56 * 2**20
        ),
        cost_estimate=pl.CostEstimate(flops=2 * 10**9, bytes_accessed=5 * 10**6, transcendentals=4 * 10**6),
        name="pair_attention",
    )(
        activations, cond_scale, cond_shift, output_gate, pair_repr, bias_weight.T, query_weight,
        query_bias, key_weight, value_weight, output_weight, token_mask,
    )


def solution(mesh):
    return jax.shard_map(
        body,
        mesh=mesh,
        in_specs=(
            P("noise", "row", None),
            P("noise", "row", None),
            P("noise", "row", None),
            P("noise", "row", None),
            P("row", "noise", None),
            P(),
            P("noise", None),
            P(),
            P("noise", None),
            P("noise", None),
            P("noise", None),
            P("noise", "row"),
        ),
        out_specs=P("noise", "row", None),
        check_vma=False,
    )
```
